256 devices in a mesh: inner: 16 (over x_hi, z), outer: 16 (over y, x_lo, core).
Axes of the slice: x: 4 (x_hi: 2, x_lo: 2; x = x_hi * 2 + x_lo), y: 4, z: 8, core: 2. Of those that a mesh axis runs over, the one named last changes fastest.
Arguments:
- queries: bfloat16 [65536, 768], P(('outer', 'inner')), may hold values from -24 to 24
- keys: bfloat16 [65536, 768], P(('outer', 'inner')), may hold values from -24 to 24
- values: bfloat16 [65536, 768], P(('outer', 'inner')), may hold values from -6 to 6
- saved_out: bfloat16 [65536, 768], P(('outer', 'inner')), may hold values from -6 to 6
- out_grad: bfloat16 [65536, 768], P(('outer', 'inner')), may hold values from -192 to 192
- offset_mid: int32 [12], replicated, may hold values from 0 to 3
- offset_wide: int32 [12], replicated, may hold values from 0 to 63
Outputs:
- query_grads: bfloat16 [65536, 768], P(('outer', 'inner'))
- key_grads: bfloat16 [65536, 768], P(('outer', 'inner'))
- value_grads: bfloat16 [65536, 768], P(('outer', 'inner'))
The draws below stay inside these ranges and needn't reach their ends.
All inputs are finite; a program needn't handle non-finite values.
Results may differ from the reference program's by a relative error of at most 0.0049.
Values may be sent and summed in bfloat16 or wider, within the bound.
A program may use at most 128 MiB of HBM per device.

```python
import math
import jax
import jax.numpy as jnp
from jax import lax

HEADS = 12
HEAD_DIM = 64
D = 768
TOK_DEV = 256
RATE_MID = 4
RATE_WIDE = 64
TOKENS = 65536
SEG_MID = 4096


def key_field(key):
    key = jax.random.fold_in(key, 12)
    fresh = jnp.clip(jax.random.normal(key, (TOKENS, D), jnp.float32), -4.0, 4.0)
    return fresh


def draw_queries(key, part):
    partner = jnp.roll(key_field(key), TOKENS // 2, axis=0)
    strength = 5.0 / HEAD_DIM ** 0.5
    key = jax.random.fold_in(key, 11)
    fresh = jnp.clip(jax.random.normal(key, (TOKENS, D), jnp.float32), -4.0, 4.0)
    mixed = jnp.clip(fresh + strength * partner, -24.0, 24.0)
    return mixed.astype(jnp.bfloat16)


def draw_keys(key, part):
    return key_field(key).astype(jnp.bfloat16)


def with_ends(result, stream_key, smallest, high):
    longest = result.shape.index(max(result.shape))
    spots = []
    for shift in (0, 1):
        where = [jax.random.randint(jax.random.fold_in(stream_key, axis), (), 0, length) for axis, length in enumerate(result.shape)]
        where[longest] = (where[longest] + shift) % result.shape[longest]
        spots.append(tuple(where))
    return result.at[spots[0]].set(smallest).at[spots[1]].set(high)


def level_of(key, shape, cuts, least, high):
    level = 1.0
    for axis_at, shards_of in cuts:
        draws = jax.random.uniform(jax.random.fold_in(jax.random.fold_in(key, 6), axis_at), (shards_of,), jnp.float32, least / len(cuts), high / len(cuts))
        level = level * jnp.repeat(jnp.exp(draws), shape[axis_at] // shards_of).reshape((-1,) + (1,) * (len(shape) - 1 - axis_at))
    return level


def noise(own_key, extent, spread, limit, shards=(), kind=jnp.bfloat16):
    result = spread * jax.random.normal(own_key, extent, jnp.float32)
    if shards:
        result = result * level_of(own_key, extent, shards, -0.22, 0.18)
    return jnp.clip(result, -limit, limit).astype(kind)


def setup_inputs(seed: int = 0) -> dict:
    key_list = jax.random.split(jax.random.key(seed), 8)
    return {
        "queries": draw_queries(jax.random.fold_in(key_list[7], 71), 0),
        "keys": draw_keys(jax.random.fold_in(key_list[7], 71), 0),
        "values": noise(key_list[2], (TOKENS, D), 1.0, 6.0, ((0, 256),)),
        "saved_out": noise(key_list[3], (TOKENS, D), 1.0, 6.0, ((0, 256),)),
        "out_grad": noise(key_list[4], (TOKENS, D), (TOK_DEV // 8), 192.0, ((0, 256),)),
        "offset_mid": with_ends(jax.random.randint(key_list[5], (HEADS,), 0, RATE_MID), jax.random.fold_in(key_list[5], 1), 0, RATE_MID - 1).astype(jnp.int32),
        "offset_wide": with_ends(jax.random.randint(key_list[6], (HEADS,), 0, RATE_WIDE), jax.random.fold_in(key_list[6], 1), 0, RATE_WIDE - 1).astype(jnp.int32),
    }


def select_rows(block, offsets, rate):
    shape = block.shape
    split = block.reshape(shape[:-3] + (shape[-3] // rate, rate) + shape[-2:])
    chosen = jnp.arange(rate, dtype=jnp.int32)[:, None] == offsets[None, :]
    return lax.optimization_barrier(jnp.sum(jnp.where(chosen[:, :, None], split, jnp.zeros((), block.dtype)), axis=-3))

def spread_rows(picked, offsets, rate):
    shape = picked.shape
    chosen = jnp.arange(rate, dtype=jnp.int32)[:, None] == offsets[None, :]
    full = jnp.where(chosen[:, :, None], jnp.expand_dims(picked, -3), jnp.zeros((), picked.dtype))
    return full.reshape(shape[:-3] + (shape[-3] * rate,) + shape[-2:])

def score_matrix_product(spec, left, right):
    return jnp.einsum(spec, left.astype(jnp.float32), right.astype(jnp.float32))

def round_bfloat(values):
    return lax.optimization_barrier(values.astype(jnp.bfloat16)).astype(jnp.float32)

def branch_lse(queries, keys, scaling_multiplier):
    logit_scores = score_matrix_product('rpj,xpj->prx', queries, keys) * scaling_multiplier
    highest = lax.optimization_barrier(jnp.max(logit_scores, axis=-1, keepdims=True))
    return jnp.transpose(highest[..., 0] + jnp.log(lax.optimization_barrier(jnp.sum(jnp.exp(logit_scores - highest), axis=-1))))

def branch_grads(queries, output_gradient, lse, deltas, keys, values, scaling_multiplier):
    logit_scores = score_matrix_product('rpj,xpj->prx', queries, keys) * scaling_multiplier
    probs = jnp.exp(logit_scores - jnp.transpose(lse)[:, :, None])
    attention_weights = round_bfloat(probs)
    value_segment_slice = score_matrix_product('vsy,svo->yvo', attention_weights, output_gradient)
    probability_gradient = score_matrix_product('rpj,xpj->prx', output_gradient, values)
    score_gradient = round_bfloat(probs * (probability_gradient - jnp.transpose(deltas)[:, :, None]))
    query_segment_slice = score_matrix_product('szr,rsx->zsx', score_gradient, keys) * scaling_multiplier
    key_segment_slice = score_matrix_product('vsy,svo->yvo', score_gradient, queries) * scaling_multiplier
    return (query_segment_slice, key_segment_slice, value_segment_slice)

def merge_lse(local, mid_full, mid_mask, wide_full, wide_mask):
    mid_value = jnp.where(mid_mask, mid_full, local)
    wide_value = jnp.where(wide_mask, wide_full, local)
    highest = jnp.maximum(local, jnp.maximum(mid_value, wide_value))
    summed = jnp.exp(local - highest)
    summed = summed + jnp.where(mid_mask, jnp.exp(mid_value - highest), 0.0)
    summed = summed + jnp.where(wide_mask, jnp.exp(wide_value - highest), 0.0)
    return highest + jnp.log(summed)

def reference(queries, keys, values, saved_out, out_grad, offset_mid, offset_wide):
    scaling_multiplier = 1.0 / math.sqrt(HEAD_DIM)
    per_head = (TOKENS, HEADS, HEAD_DIM)
    query_rows = queries.reshape(per_head)
    key_rows = keys.reshape(per_head)
    value_rows = values.reshape(per_head)
    grad_rows = out_grad.reshape(per_head)
    deltas = lax.optimization_barrier(jnp.sum(grad_rows.astype(jnp.float32) * saved_out.reshape(per_head).astype(jnp.float32), axis=-1))
    local_count = TOKENS // TOK_DEV
    mid_count = TOKENS // SEG_MID

    def local_view(block):
        return block.reshape((local_count, TOK_DEV) + block.shape[1:])

    def mid_view(block):
        return select_rows(block.reshape((mid_count, SEG_MID) + block.shape[1:]), offset_mid, RATE_MID)

    def wide_view(block):
        return select_rows(block, offset_wide, RATE_WIDE)
    lse_local = lax.map(lambda operands: branch_lse(operands[0], operands[1], scaling_multiplier), (local_view(query_rows), local_view(key_rows))).reshape(TOKENS, HEADS)
    query_mid, key_mid, value_mid, grad_mid = [mid_view(block) for block in (query_rows, key_rows, value_rows, grad_rows)]
    lse_mid = lax.map(lambda operands: branch_lse(operands[0], operands[1], scaling_multiplier), (query_mid, key_mid))
    query_wide, key_wide, value_wide, grad_wide = [wide_view(block) for block in (query_rows, key_rows, value_rows, grad_rows)]
    lse_wide = branch_lse(query_wide, key_wide, scaling_multiplier)
    position = jnp.arange(TOKENS, dtype=jnp.int32)
    mid_mask = (position % RATE_MID)[:, None] == offset_mid[None, :]
    wide_mask = (position % RATE_WIDE)[:, None] == offset_wide[None, :]
    mid_full = spread_rows(lse_mid[..., None], offset_mid, RATE_MID).reshape(TOKENS, HEADS)
    wide_full = spread_rows(lse_wide[..., None], offset_wide, RATE_WIDE).reshape(TOKENS, HEADS)
    lse_total = merge_lse(lse_local, mid_full, mid_mask, wide_full, wide_mask)
    lse_mid_rows = mid_view(lse_total[..., None])[..., 0]
    delta_mid_rows = mid_view(deltas[..., None])[..., 0]
    lse_wide_rows = wide_view(lse_total[..., None])[..., 0]
    delta_wide_rows = wide_view(deltas[..., None])[..., 0]

    def grads_step(operands):
        return branch_grads(operands[0], operands[1], operands[2], operands[3], operands[4], operands[5], scaling_multiplier)
    local_parts = lax.map(grads_step, (local_view(query_rows), local_view(grad_rows), local_view(lse_total), local_view(deltas), local_view(key_rows), local_view(value_rows)))
    mid_parts = lax.map(grads_step, (query_mid, grad_mid, lse_mid_rows, delta_mid_rows, key_mid, value_mid))
    wide_parts = branch_grads(query_wide, grad_wide, lse_wide_rows, delta_wide_rows, key_wide, value_wide, scaling_multiplier)
    results = []
    for index in range(3):
        summed = local_parts[index].reshape(per_head)
        summed = summed + spread_rows(mid_parts[index], offset_mid, RATE_MID).reshape(per_head)
        summed = summed + spread_rows(wide_parts[index], offset_wide, RATE_WIDE).reshape(per_head)
        results.append(summed.astype(jnp.bfloat16).reshape(TOKENS, D))
    return (results[0], results[1], results[2])
```

```python
import jax
import jax.numpy as jnp
from jax import lax
from jax.experimental import pallas as pl
from jax.experimental.pallas import tpu as pltpu
from jax.sharding import PartitionSpec as P

BF = jnp.bfloat16
F32 = jnp.float32
I32 = jnp.int32

N = 16
HEADS = 12
T = 256
MID = 64
SCALE = 0.125
NEG = -1e30
MSG = 144
RET = 96


def iota(shape, dim):
    return lax.broadcasted_iota(I32, shape, dim)


def nn(a, b):
    return lax.dot_general(a, b, (((1,), (0,)), ((), ())), preferred_element_type=F32)


def nt(a, b):
    return lax.dot_general(a, b, (((1,), (1,)), ((), ())), preferred_element_type=F32)


def tn(a, b):
    return lax.dot_general(a, b, (((0,), (0,)), ((), ())), preferred_element_type=F32)


def onehot(mask):
    return jnp.where(mask, 1.0, 0.0).astype(BF)


def split3(x):
    a = x.astype(BF).astype(F32)
    r = x - a
    b = r.astype(BF).astype(F32)
    return jnp.concatenate([a, b, r - b], axis=0).astype(BF)


def sum3(x):
    r = x.shape[0] // 3
    return x[:r] + x[r : 2 * r] + x[2 * r :]


def lse3(a, b, c):
    top = jnp.maximum(a, jnp.maximum(b, c))
    return top + jnp.log(jnp.exp(a - top) + jnp.exp(b - top) + jnp.exp(c - top))


def swap(x):
    return pltpu.roll(x, 64, 1)


def device_of(h):
    return (h // 3) * 4 + h % 3


def kernel(
    om_ref, ow_ref, q_ref, k_ref, v_ref, o_ref, g_ref,
    dq_ref, dk_ref, dv_ref,
    xl, yl, msg, rx, el, gl, mst, st_tx, st_rx, ls_tx, ls_rx,
    yk, yv, s_scr, em, gm, mm, ml, dm, xw_all, xw_w, yw, rxo, wp, rxp,
    ret, retw, ret_rx, retw_rx, acc_kv, acc_q,
    msg_s, msg_r, st_s, st_r, ls_s, ls_r, yw_s, yw_r, wp_s, wp_r, ret_s, ret_r, retw_s, retw_r,
):
    inner = lax.axis_index("inner")
    outer = lax.axis_index("outer")
    active = inner % 4 < 3
    head = jnp.minimum((inner // 4) * 3 + inner % 4, HEADS - 1)

    def to_inner(src, dst, send, recv, target):
        return pltpu.make_async_remote_copy(
            src_ref=src, dst_ref=dst, send_sem=send, recv_sem=recv,
            device_id={"inner": target}, device_id_type=pl.DeviceIdType.MESH,
        )

    def to_outer(src, dst, send, recv, target):
        return pltpu.make_async_remote_copy(
            src_ref=src, dst_ref=dst, send_sem=send, recv_sem=recv,
            device_id={"outer": target}, device_id_type=pl.DeviceIdType.MESH,
        )

    barrier = pltpu.get_barrier_semaphore()

    def greet(d, _):
        pl.semaphore_signal(
            barrier, inc=1, device_id={"inner": (inner + d) % N}, device_id_type=pl.DeviceIdType.MESH
        )
        pl.semaphore_signal(
            barrier, inc=1, device_id={"outer": (outer + d) % N}, device_id_type=pl.DeviceIdType.MESH
        )
        return 0

    lax.fori_loop(1, N, greet, 0)

    left = iota((1, 128), 1) < 64
    half_k = jnp.where(left, SCALE, 0.0).astype(BF)
    half_v = jnp.where(left, 0.0, 1.0).astype(BF)

    def order(step):
        return (step + inner) % (HEADS // 2)

    def pack(step, _):
        p = order(step)
        cols = pl.ds(pl.multiple_of(p * 128, 128), 128)
        qp, kp, vp, gp = q_ref[:, cols], k_ref[:, cols], v_ref[:, cols], g_ref[:, cols]
        for a in range(2):
            h = 2 * p + a
            lo, hi = 64 * a, 64 * a + 64
            x = jnp.concatenate([qp[:, lo:hi], gp[:, lo:hi]], axis=1)
            y = jnp.concatenate([kp[:, lo:hi], vp[:, lo:hi]], axis=1)
            xl[h] = x
            yl[h] = y
            om, ow = om_ref[h], ow_ref[h]
            row = iota((96, 1), 0)
            r = row - 64
            w = r & 15
            wide = jnp.where((r < 16) & (w < 4), 64 * w + ow, -1)
            wide = jnp.where((r >= 16) & (w >= 4) & (w < 8), 64 * (w - 4) + ow, wide)
            want = jnp.where(row < 64, 4 * row + om, wide)
            pick = onehot(iota((96, T), 1) == want)
            got = nn(pick, jnp.concatenate([x, y], axis=1))
            msg[h, 0:64, :] = got[0:64, 0:128].astype(BF)
            msg[h, 64:128, :] = got[0:64, 128:256].astype(BF)
            msg[h, 128:144, :] = (got[64:80, 0:128] + got[80:96, 128:256]).astype(BF)
        return 0

    lax.fori_loop(0, HEADS // 2, pack, 0)
    pl.semaphore_wait(barrier, 2 * (N - 1))

    def send_msg(step, _):
        h = (step + 2 * inner) % HEADS
        target = device_of(h)

        @pl.when(target != inner)
        def _():
            to_inner(msg.at[h], rx.at[inner], msg_s.at[h], msg_r.at[inner], target).start()

        @pl.when(target == inner)
        def _():
            rx[inner] = msg[h]

        return 0

    lax.fori_loop(0, HEADS, send_msg, 0)

    t_row = iota((T, 128), 0)
    t_lane = iota((T, 128), 1)
    place_m = onehot(t_lane == (t_row >> 2) + 64 * (inner % 2))
    place_w = onehot(t_lane == (t_row >> 6) + 4 * inner)
    tok = iota((1, T), 1)

    def local_a(p, _):
        cols = pl.ds(pl.multiple_of(p * 128, 128), 128)
        prod = g_ref[:, cols].astype(F32) * o_ref[:, cols].astype(F32)
        hi = prod.astype(BF)
        lo = (prod - hi.astype(F32)).astype(BF)
        halves = onehot(iota((16, 128), 0) == (iota((16, 128), 1) >> 6))
        delta = nt(halves, hi) + nt(halves, lo)
        tops, lses = [], []
        for a in range(2):
            h = 2 * p + a
            x, y = xl[h], yl[h]
            s = nt(y * half_k, x)
            top = jnp.max(s, axis=0, keepdims=True)
            e = jnp.exp(s - top)
            tops.append(top)
            lses.append(top + jnp.log(jnp.sum(e, axis=0, keepdims=True)))
            d = nt(y * half_v, x)
            el[h] = e.astype(BF)
            gl[h] = (e * (d - delta[a : a + 1])).astype(BF)
        row = iota((8, 1), 0)
        mst[p] = jnp.where(
            row < 2, jnp.where(row == 0, tops[0], tops[1]), jnp.where(row == 2, lses[0], lses[1])
        )
        first, wide = row < 4, (row & 2) != 0
        is_delta = (row & 1) == 0
        base = jnp.where(
            first,
            jnp.where(is_delta, delta[0:1], lses[0]),
            jnp.where(is_delta, delta[1:2], lses[1]),
        )
        off = jnp.where(
            first,
            jnp.where(wide, ow_ref[2 * p], om_ref[2 * p]),
            jnp.where(wide, ow_ref[2 * p + 1], om_ref[2 * p + 1]),
        )
        kept = (tok & jnp.where(wide, 63, 3)) == off
        parts = split3(jnp.where(kept, base, 0.0))
        st_tx[p] = jnp.where(wide, sum3(nn(parts, place_w)), sum3(nn(parts, place_m)))
        return 0

    lax.fori_loop(0, HEADS // 2, local_a, 0)

    def send_st(step, _):
        h = (step + 2 * inner) % HEADS
        target = device_of(h)

        @pl.when(target != inner)
        def _():
            to_inner(st_tx.at[h // 2], st_rx.at[inner], st_s.at[h], st_r.at[inner], target).start()

        @pl.when(target == inner)
        def _():
            st_rx[inner] = st_tx[h // 2]

        return 0

    lax.fori_loop(0, HEADS, send_st, 0)

    @pl.when(active)
    def _():
        def get_msg(i, _):
            @pl.when(i != inner)
            def _():
                to_inner(msg.at[0], rx.at[i], msg_s.at[0], msg_r.at[i], i).wait_recv()

            return 0

        lax.fori_loop(0, N, get_msg, 0)

        om, ow = om_ref[head], ow_ref[head]
        row64, col256 = iota((64, T), 0), iota((64, T), 1)
        at = 16 * (row64 >> 2) + (row64 & 3)
        wide_rows = rx[:, 128:144, :].reshape(T, 128)
        xw_w[...] = nn(onehot(col256 == at), wide_rows).astype(BF)
        yw[...] = nn(onehot(col256 == at + 4), wide_rows).astype(BF)
        rxo[outer] = yw[...]

        def send_yw(d, _):
            t = (outer + d) % N
            to_outer(yw, rxo.at[outer], yw_s.at[t], yw_r.at[outer], t).start()
            return 0

        lax.fori_loop(1, N, send_yw, 0)

        def get_st(i, _):
            @pl.when(i != inner)
            def _():
                to_inner(st_tx.at[0], st_rx.at[i], st_s.at[0], st_r.at[i], i).wait_recv()

            return 0

        lax.fori_loop(0, N, get_st, 0)

        even = head % 2 == 0

        def stat(index):
            return jnp.where(even, st_rx[:, index, :], st_rx[:, index + 4, :])

        def chunks(rows):
            pair = iota((8, N), 0) == (iota((8, N), 1) >> 1)
            return sum3_cols(pair, rows)

        def sum3_cols(pair, rows):
            a = rows.astype(BF).astype(F32)
            r = rows - a
            b = r.astype(BF).astype(F32)
            c = (r - b).astype(BF)
            ones = onehot(pair)
            return nn(ones, a.astype(BF)) + nn(ones, b.astype(BF)) + nn(ones, c)

        dm[...] = chunks(stat(0))
        lse_local_m = chunks(stat(1))
        delta_w = jnp.sum(stat(2), axis=0, keepdims=True)
        lse_local_w = jnp.sum(stat(3), axis=0, keepdims=True)

        def halves(i, _):
            y = rx[i, 64:128, :]
            yk[i] = y * half_k
            yv[i] = y * half_v
            return 0

        lax.fori_loop(0, N, halves, 0)

        def mid_a(b, _):
            x = rx[pl.ds(4 * b, 4), 0:64, :].reshape(T, 128)
            delta = jnp.concatenate([dm[pl.ds(2 * b, 1), :], dm[pl.ds(2 * b + 1, 1), :]], axis=1)
            top = jnp.full((1, T), NEG, F32)
            for kb in range(4):
                s = nt(yk[4 * kb : 4 * kb + 4].reshape(T, 128), x)
                s_scr[kb] = s
                top = jnp.maximum(top, jnp.max(s, axis=0, keepdims=True))
            total = jnp.zeros((1, T), F32)
            for kb in range(4):
                e = jnp.exp(s_scr[kb] - top)
                total = total + jnp.sum(e, axis=0, keepdims=True)
                d = nt(yv[4 * kb : 4 * kb + 4].reshape(T, 128), x)
                em[b, kb] = e.astype(BF)
                gm[b, kb] = (e * (d - delta)).astype(BF)
            lse = top + jnp.log(total)
            mm[pl.ds(2 * b, 1), :] = top[:, :128]
            mm[pl.ds(2 * b + 1, 1), :] = top[:, 128:]
            ml[pl.ds(2 * b, 1), :] = lse[:, :128]
            ml[pl.ds(2 * b + 1, 1), :] = lse[:, 128:]
            return 0

        lax.fori_loop(0, 4, mid_a, 0)

        def get_yw(i, _):
            @pl.when(i != outer)
            def _():
                to_outer(yw, rxo.at[i], yw_s.at[i], yw_r.at[i], i).wait_recv()

            return 0

        lax.fori_loop(0, N, get_yw, 0)

        all_y = rxo[...].reshape(N * 64, 128)
        x_w = xw_w[...]
        s = nt(all_y * half_k, x_w)
        top_w = jnp.max(s, axis=0, keepdims=True)
        e = jnp.exp(s - top_w)
        lse_w = top_w + jnp.log(jnp.sum(e, axis=0, keepdims=True))
        d = nt(all_y * half_v, x_w)
        ew = e.astype(BF)
        gw = (e * (d - delta_w[:, :64])).astype(BF)
        zeros64 = jnp.zeros((1, 64), F32)
        top_w = jnp.concatenate([top_w, zeros64], axis=1)
        lse_w = jnp.concatenate([lse_w, zeros64], axis=1)

        lse_m = ml[...]
        shared = (ow & 3) == om
        spot = jnp.where(shared, ow >> 2, -1)
        lane8, chunk8 = iota((8, 128), 1), iota((8, 128), 0)
        here = (lane8 & 15) == spot
        n128 = iota((128, 128), 1)
        spread = onehot(((n128 & 7) == (iota((128, 128), 0) >> 4)) & (n128 < 64))
        own = (lane8 >> 3) == chunk8
        m_at_w = sum3(nn(split3(jnp.where(here, lse_m, 0.0)), spread))
        m_at_w = jnp.sum(jnp.where(own, m_at_w, 0.0), axis=0, keepdims=True)
        w_at_m = sum3(nt(split3(jnp.where(own, lse_w, 0.0)), spread))
        total_m = lse3(lse_m, lse_local_m, jnp.where(here, w_at_m, NEG))
        spot_row = jnp.full((1, 128), spot, I32)
        total_w = lse3(lse_w, lse_local_w, jnp.where(spot_row >= 0, m_at_w, NEG))
        for j in range(8):
            ls_tx[j] = jnp.where(chunk8 == 0, lse_m[j : j + 1], lse_w)

        def send_ls(d, _):
            t = (inner + d) % N
            to_inner(ls_tx.at[t // 2], ls_rx.at[head], ls_s.at[t], ls_r.at[head], t).start()
            return 0

        lax.fori_loop(1, N, send_ls, 0)
        ls_rx[head] = ls_tx[inner // 2]

        weight_m = jnp.exp(mm[...] - total_m)
        weight_w = jnp.exp(top_w - total_w)
        stacked = jnp.concatenate(
            [weight_m, jnp.broadcast_to(weight_w, (8, 128)), jnp.zeros((112, 128), F32)], axis=0
        )
        columns = stacked.T

        col_w = columns[0:64, 8:9]
        scaled = (x_w.astype(F32) * col_w).astype(BF)
        wp[...] = jnp.where(left, nn(gw, scaled), nn(ew, scaled)).astype(BF).reshape(N, 64, 128)
        rxp[outer] = wp[outer]

        def send_wp(d, _):
            t = (outer + d) % N
            to_outer(wp.at[t], rxp.at[outer], wp_s.at[t], wp_r.at[outer], t).start()
            return 0

        lax.fori_loop(1, N, send_wp, 0)
        dq_w = (tn(gw, all_y) * col_w).astype(BF)

        for j in range(8):
            x = rx[2 * j : 2 * j + 2, 0:64, :].reshape(128, 128).astype(F32)
            col = columns[:, j : j + 1]
            xw_all[128 * j : 128 * j + 128, :] = (x * col).astype(BF)
            acc_q[0, 128 * j % 256 : 128 * j % 256 + 128, :] = jnp.broadcast_to(col, (128, 128))
            if j % 2 == 1:
                b = j // 2
                g_k = jnp.zeros((T, 128), F32)
                for kb in range(4):
                    g_k = g_k + tn(gm[b, kb], rx[4 * kb : 4 * kb + 4, 64:128, :].reshape(T, 128))
                g_k = g_k * acc_q[0]
                for i in range(4):
                    mine = g_k[64 * i : 64 * i + 64]
                    ret[4 * b + i, 64:96, :] = jnp.where(left, mine[:32], swap(mine[32:])).astype(BF)

        def mid_b(kb, _):
            from_g = jnp.zeros((T, 128), F32)
            from_e = jnp.zeros((T, 128), F32)
            for b in range(4):
                x = xw_all[256 * b : 256 * b + 256, :]
                from_g = from_g + nn(gm[b, kb], x)
                from_e = from_e + nn(em[b, kb], x)
            both = jnp.where(left, from_g, from_e).astype(BF)
            ret[pl.ds(4 * kb, 4), 0:64, :] = both.reshape(4, 64, 128)
            for i in range(4):
                t = 4 * kb + i

                @pl.when(t != inner)
                def _():
                    to_inner(ret.at[t], ret_rx.at[head], ret_s.at[t], ret_r.at[head], t).start()

            return 0

        lax.fori_loop(0, 4, mid_b, 0)
        ret_rx[head] = ret[inner]

        def get_wp(i, total):
            @pl.when(i != outer)
            def _():
                to_outer(wp.at[0], rxp.at[i], wp_s.at[0], wp_r.at[i], i).wait_recv()

            return total + rxp[i].astype(F32)

        kv_w = lax.fori_loop(0, N, get_wp, jnp.zeros((64, 128), F32)).astype(BF)
        r256, n64 = iota((T, 64), 0), iota((T, 64), 1)
        slot = r256 & 15
        at = 4 * (r256 >> 4) + (slot & 3)
        back = nn(onehot((n64 == at) & (slot < 4)), kv_w)
        back = back + nn(onehot((n64 == at) & (slot >= 4) & (slot < 8)), dq_w)
        retw[...] = back.astype(BF).reshape(N, 16, 128)

        def send_retw(d, _):
            t = (inner + d) % N
            to_inner(retw.at[t], retw_rx.at[head], retw_s.at[t], retw_r.at[head], t).start()
            return 0

        lax.fori_loop(1, N, send_retw, 0)
        retw_rx[head] = retw[inner]

    def get_ls(h, _):
        t = device_of(h)

        @pl.when(t != inner)
        def _():
            to_inner(ls_tx.at[0], ls_rx.at[h], ls_s.at[0], ls_r.at[h], t).wait_recv()

        return 0

    lax.fori_loop(0, HEADS, get_ls, 0)

    def local_b(p, _):
        row = iota((8, 1), 0)
        first, second = ls_rx[2 * p], ls_rx[2 * p + 1]
        rows = jnp.where(
            row < 2,
            jnp.where(row == 0, first[0:1], second[0:1]),
            jnp.where(row == 2, first[1:2], second[1:2]),
        )
        parts = split3(rows)
        lse_m = sum3(nt(parts, place_m))[0:2]
        lse_w = sum3(nt(parts, place_w))[2:4]
        top, lse = mst[p][0:2], mst[p][2:4]
        row2 = iota((2, 1), 0)
        om = jnp.where(row2 == 0, om_ref[2 * p], om_ref[2 * p + 1])
        ow = jnp.where(row2 == 0, ow_ref[2 * p], ow_ref[2 * p + 1])
        total = lse3(
            lse, jnp.where((tok & 3) == om, lse_m, NEG), jnp.where((tok & 63) == ow, lse_w, NEG)
        )
        weight = jnp.exp(top - total)
        r128 = iota((128, 1), 0)
        columns = jnp.where(r128 == 0, weight[0:1], weight[1:2]).T
        for a in range(2):
            h = 2 * p + a
            col = columns[:, a : a + 1]
            x = (xl[h].astype(F32) * col).astype(BF)
            acc_kv[h] = jnp.where(left, nn(gl[h], x), nn(el[h], x))
            acc_q[h] = tn(gl[h], yl[h]) * col
        return 0

    lax.fori_loop(0, HEADS // 2, local_b, 0)

    def get_ret(h, _):
        t = device_of(h)

        @pl.when(t != inner)
        def _():
            to_inner(ret.at[0], ret_rx.at[h], ret_s.at[0], ret_r.at[h], t).wait_recv()
            to_inner(retw.at[0], retw_rx.at[h], retw_s.at[0], retw_r.at[h], t).wait_recv()

        return 0

    lax.fori_loop(0, HEADS, get_ret, 0)

    def finish(p, _):
        cols = pl.ds(pl.multiple_of(p * 128, 128), 128)
        kvs, qs, rest = [], [], []
        for a in range(2):
            h = 2 * p + a
            om, ow = om_ref[h], ow_ref[h]
            r = iota((1, 112), 1)
            t = iota((T, 112), 0)
            back = jnp.concatenate([ret_rx[h], retw_rx[h]], axis=0)
            want_kv = jnp.where(r < 64, 4 * r + om, jnp.where((r >= 96) & (r < 100), 64 * (r - 96) + ow, -1))
            in_q = (r >= 64) & (r < 96)
            want_q = jnp.where(
                in_q, 4 * (r - 64) + om, jnp.where((r >= 100) & (r < 104), 64 * (r - 100) + ow, -1)
            )
            want_r = jnp.where(in_q, 4 * (r - 32) + om, -1)
            kvs.append(acc_kv[h] + nn(onehot(t == want_kv), back))
            qs.append(acc_q[h] + nn(onehot(t == want_q), back))
            rest.append(nn(onehot(t == want_r), back))
        dq = jnp.where(left, qs[0] + swap(rest[0]), swap(qs[1]) + rest[1])
        dq_ref[:, cols] = (SCALE * dq).astype(BF)
        dk_ref[:, cols] = (SCALE * jnp.where(left, kvs[0], swap(kvs[1]))).astype(BF)
        dv_ref[:, cols] = jnp.where(left, swap(kvs[0]), kvs[1]).astype(BF)
        return 0

    lax.fori_loop(0, HEADS // 2, finish, 0)

    def sent_heads(h, _):
        t = device_of(h)

        @pl.when(t != inner)
        def _():
            to_inner(msg.at[h], rx.at[inner], msg_s.at[h], msg_r.at[inner], t).wait_send()
            to_inner(st_tx.at[h // 2], st_rx.at[inner], st_s.at[h], st_r.at[inner], t).wait_send()

        return 0

    lax.fori_loop(0, HEADS, sent_heads, 0)

    @pl.when(active)
    def _():
        def sent(d, _):
            t = (inner + d) % N
            to_inner(ls_tx.at[t // 2], ls_rx.at[head], ls_s.at[t], ls_r.at[head], t).wait_send()
            to_inner(ret.at[t], ret_rx.at[head], ret_s.at[t], ret_r.at[head], t).wait_send()
            to_inner(retw.at[t], retw_rx.at[head], retw_s.at[t], retw_r.at[head], t).wait_send()
            t = (outer + d) % N
            to_outer(yw, rxo.at[outer], yw_s.at[t], yw_r.at[outer], t).wait_send()
            to_outer(wp.at[t], rxp.at[outer], wp_s.at[t], wp_r.at[outer], t).wait_send()
            return 0

        lax.fori_loop(1, N, sent, 0)


def per_device(queries, keys, values, saved_out, out_grad, offset_mid, offset_wide):
    out = jax.ShapeDtypeStruct((T, HEADS * 64), BF)
    vmem = pl.BlockSpec(memory_space=pltpu.VMEM)
    smem = pl.BlockSpec(memory_space=pltpu.SMEM)
    v = pltpu.VMEM
    dma = pltpu.SemaphoreType.DMA
    return pl.pallas_call(
        kernel,
        out_shape=(out, out, out),
        in_specs=[smem, smem] + [vmem] * 5,
        out_specs=(vmem, vmem, vmem),
        scratch_shapes=[
            v((HEADS, T, 128), BF),
            v((HEADS, T, 128), BF),
            v((HEADS, MSG, 128), BF),
            v((N, MSG, 128), BF),
            v((HEADS, T, T), BF),
            v((HEADS, T, T), BF),
            v((HEADS // 2, 8, T), F32),
            v((HEADS // 2, 8, 128), F32),
            v((N, 8, 128), F32),
            v((8, 8, 128), F32),
            v((HEADS, 8, 128), F32),
            v((N, 64, 128), BF),
            v((N, 64, 128), BF),
            v((4, T, T), F32),
            v((4, 4, T, T), BF),
            v((4, 4, T, T), BF),
            v((8, 128), F32),
            v((8, 128), F32),
            v((8, 128), F32),
            v((N * 64, 128), BF),
            v((64, 128), BF),
            v((64, 128), BF),
            v((N, 64, 128), BF),
            v((N, 64, 128), BF),
            v((N, 64, 128), BF),
            v((N, RET, 128), BF),
            v((N, 16, 128), BF),
            v((HEADS, RET, 128), BF),
            v((HEADS, 16, 128), BF),
            v((HEADS, T, 128), F32),
            v((HEADS, T, 128), F32),
            dma((HEADS,)), dma((N,)),
            dma((HEADS,)), dma((N,)),
            dma((N,)), dma((HEADS,)),
            dma((N,)), dma((N,)),
            dma((N,)), dma((N,)),
            dma((N,)), dma((HEADS,)),
            dma((N,)), dma((HEADS,)),
        ],
        compiler_params=pltpu.CompilerParams(
            collective_id=0, has_side_effects=True, vmem_limit_bytes=48 * 1024 * 1024
        ),
    )(offset_mid, offset_wide, queries, keys, values, saved_out, out_grad)


def solution(mesh):
    rows = P(("outer", "inner"), None)
    return jax.shard_map(
        per_device,
        mesh=mesh,
        in_specs=(rows, rows, rows, rows, rows, P(), P()),
        out_specs=(rows, rows, rows),
        check_vma=False,
    )
```

```python
import jax
import jax.numpy as jnp
from jax import lax
from jax.experimental import pallas as pl
from jax.experimental.pallas import tpu as pltpu
from jax.sharding import PartitionSpec as P

BF = jnp.bfloat16
F32 = jnp.float32
I32 = jnp.int32

N = 16
HEADS = 12
T = 256
MID = 64
SCALE = 0.125
NEG = -1e30
BACK = 112


def iota(shape, dim):
    return lax.broadcasted_iota(I32, shape, dim)


def nn(a, b):
    return lax.dot_general(a, b, (((1,), (0,)), ((), ())), preferred_element_type=F32)


def nt(a, b):
    return lax.dot_general(a, b, (((1,), (1,)), ((), ())), preferred_element_type=F32)


def tn(a, b):
    return lax.dot_general(a, b, (((0,), (0,)), ((), ())), preferred_element_type=F32)


def onehot(mask):
    return jnp.where(mask, 1.0, 0.0).astype(BF)


def split3(x):
    a = x.astype(BF).astype(F32)
    r = x - a
    b = r.astype(BF).astype(F32)
    return jnp.concatenate([a, b, r - b], axis=0).astype(BF)


def sum3(x):
    r = x.shape[0] // 3
    return x[:r] + x[r : 2 * r] + x[2 * r :]


def lse3(a, b, c):
    top = jnp.maximum(a, jnp.maximum(b, c))
    return top + jnp.log(jnp.exp(a - top) + jnp.exp(b - top) + jnp.exp(c - top))


def swap(x):
    return pltpu.roll(x, 64, 1)


def device_of(h):
    return (h // 3) * 4 + h % 3


def kernel(
    om_hbm, ow_hbm, q_hbm, k_hbm, v_hbm, o_hbm, g_hbm,
    acc_kv, acc_q, back, where_back,
    om_ref, ow_ref, q_ref, k_ref, v_ref, o_ref, g_ref,
    xl, yl, msg_w, msg_k, msg_q, rx_w, rx_k, rx_q, el, gl, mst, st_tx, st_rx, ls_tx, ls_rx,
    yk, yv, s_scr, em, gm, mm, ml, dm, dq_m, xw_all, xw_w, yw, rxo, wp, rxp, ret, retw,
    in_s, mw_s, mw_r, mk_s, mk_r, mq_s, mq_r, st_s, st_r, ls_s, ls_r, yw_s, yw_r, wp_s, wp_r,
    rk_s, rk_r, rq_s, rq_r, rw_s, rw_r,
):
    inner = lax.axis_index("inner")
    outer = lax.axis_index("outer")
    quad = inner // 4
    active = inner % 4 < 3
    head = jnp.minimum(quad * 3 + inner % 4, HEADS - 1)

    def to_inner(src, dst, send, recv, target):
        return pltpu.make_async_remote_copy(
            src_ref=src, dst_ref=dst, send_sem=send, recv_sem=recv,
            device_id={"inner": target}, device_id_type=pl.DeviceIdType.MESH,
        )

    def to_outer(src, dst, send, recv, target):
        return pltpu.make_async_remote_copy(
            src_ref=src, dst_ref=dst, send_sem=send, recv_sem=recv,
            device_id={"outer": target}, device_id_type=pl.DeviceIdType.MESH,
        )

    loads = [
        pltpu.make_async_copy(src, dst, in_s.at[i])
        for i, (src, dst) in enumerate(
            [
                (om_hbm, om_ref), (ow_hbm, ow_ref), (q_hbm, q_ref), (g_hbm, g_ref),
                (k_hbm, k_ref), (v_hbm, v_ref), (o_hbm, o_ref),
            ]
        )
    ]
    for load in loads:
        load.start()

    barrier = pltpu.get_barrier_semaphore()

    def greet(d, _):
        pl.semaphore_signal(
            barrier, inc=1, device_id={"inner": (inner + d) % N}, device_id_type=pl.DeviceIdType.MESH
        )
        pl.semaphore_signal(
            barrier, inc=1, device_id={"outer": (outer + d) % N}, device_id_type=pl.DeviceIdType.MESH
        )
        return 0

    lax.fori_loop(1, N, greet, 0)
    for load in loads[:6]:
        load.wait()

    left = iota((1, 128), 1) < 64
    half_k = jnp.where(left, SCALE, 0.0).astype(BF)
    half_v = jnp.where(left, 0.0, 1.0).astype(BF)

    def pack(p, _):
        cols = pl.ds(pl.multiple_of(p * 128, 128), 128)
        qp, kp, vp, gp = q_ref[:, cols], k_ref[:, cols], v_ref[:, cols], g_ref[:, cols]
        for a in range(2):
            h = 2 * p + a
            lo, hi = 64 * a, 64 * a + 64
            x = jnp.concatenate([qp[:, lo:hi], gp[:, lo:hi]], axis=1)
            y = jnp.concatenate([kp[:, lo:hi], vp[:, lo:hi]], axis=1)
            xl[h] = x
            yl[h] = y
            om, ow = om_ref[h], ow_ref[h]
            row = iota((96, 1), 0)
            r = row - 64
            w = r & 15
            wide = jnp.where((r < 16) & (w < 4), 64 * w + ow, -1)
            wide = jnp.where((r >= 16) & (w >= 4) & (w < 8), 64 * (w - 4) + ow, wide)
            want = jnp.where(row < 64, 4 * row + om, wide)
            pick = onehot(iota((96, T), 1) == want)
            got = nn(pick, jnp.concatenate([x, y], axis=1))
            msg_q[h] = got[0:64, 0:128].astype(BF)
            msg_k[h] = got[0:64, 128:256].astype(BF)
            msg_w[h] = (got[64:80, 0:128] + got[80:96, 128:256]).astype(BF)
        return 0

    lax.fori_loop(0, HEADS // 2, pack, 0)
    pl.semaphore_wait(barrier, 2 * (N - 1))

    def send_to_heads(src_of, dst, send, recv):
        def step(i, _):
            block = (quad + i // 3) % 4
            j = (i + inner) % 3
            h, target = 3 * block + j, 4 * block + j

            @pl.when(target != inner)
            def _():
                to_inner(src_of(h), dst.at[inner], send.at[h], recv.at[inner], target).start()

            return 0

        lax.fori_loop(0, HEADS, step, 0)

    send_to_heads(lambda h: msg_w.at[h], rx_w, mw_s, mw_r)
    send_to_heads(lambda h: msg_k.at[h], rx_k, mk_s, mk_r)
    send_to_heads(lambda h: msg_q.at[h], rx_q, mq_s, mq_r)

    @pl.when(active)
    def _():
        rx_w[inner] = msg_w[head]
        rx_k[inner] = msg_k[head]
        rx_q[inner] = msg_q[head]

    t_row = iota((T, 128), 0)
    t_lane = iota((T, 128), 1)
    place_m = onehot(t_lane == (t_row >> 2) + 64 * (inner % 2))
    place_w = onehot(t_lane == (t_row >> 6) + 4 * inner)
    tok = iota((1, T), 1)
    loads[6].wait()

    def local_a(p, _):
        cols = pl.ds(pl.multiple_of(p * 128, 128), 128)
        prod = g_ref[:, cols].astype(F32) * o_ref[:, cols].astype(F32)
        hi = prod.astype(BF)
        lo = (prod - hi.astype(F32)).astype(BF)
        halves = onehot(iota((16, 128), 0) == (iota((16, 128), 1) >> 6))
        delta = nt(halves, hi) + nt(halves, lo)
        tops, lses = [], []
        for a in range(2):
            h = 2 * p + a
            x, y = xl[h], yl[h]
            s = nt(y * half_k, x)
            top = jnp.max(s, axis=0, keepdims=True)
            e = jnp.exp(s - top)
            tops.append(top)
            lses.append(top + jnp.log(jnp.sum(e, axis=0, keepdims=True)))
            d = nt(y * half_v, x)
            el[h] = e.astype(BF)
            gl[h] = (e * (d - delta[a : a + 1])).astype(BF)
        row = iota((8, 1), 0)
        mst[p] = jnp.where(
            row < 2, jnp.where(row == 0, tops[0], tops[1]), jnp.where(row == 2, lses[0], lses[1])
        )
        first, wide = row < 4, (row & 2) != 0
        is_delta = (row & 1) == 0
        base = jnp.where(
            first,
            jnp.where(is_delta, delta[0:1], lses[0]),
            jnp.where(is_delta, delta[1:2], lses[1]),
        )
        off = jnp.where(
            first,
            jnp.where(wide, ow_ref[2 * p], om_ref[2 * p]),
            jnp.where(wide, ow_ref[2 * p + 1], om_ref[2 * p + 1]),
        )
        kept = (tok & jnp.where(wide, 63, 3)) == off
        parts = split3(jnp.where(kept, base, 0.0))
        st_tx[p] = jnp.where(wide, sum3(nn(parts, place_w)), sum3(nn(parts, place_m)))
        return 0

    lax.fori_loop(0, HEADS // 2, local_a, 0)
    send_to_heads(lambda h: st_tx.at[h // 2], st_rx, st_s, st_r)

    @pl.when(active)
    def _():
        st_rx[inner] = st_tx[head // 2]

        def get_wide(i, _):
            @pl.when(i != inner)
            def _():
                to_inner(msg_w.at[0], rx_w.at[i], mw_s.at[0], mw_r.at[i], i).wait_recv()

            return 0

        lax.fori_loop(0, N, get_wide, 0)
        row64, col256 = iota((64, T), 0), iota((64, T), 1)
        at = 16 * (row64 >> 2) + (row64 & 3)
        wide_rows = rx_w[...].reshape(T, 128)
        xw_w[...] = nn(onehot(col256 == at), wide_rows).astype(BF)
        yw[...] = nn(onehot(col256 == at + 4), wide_rows).astype(BF)
        rxo[outer] = yw[...]

        def send_yw(d, _):
            t = (outer + d) % N
            to_outer(yw, rxo.at[outer], yw_s.at[t], yw_r.at[outer], t).start()
            return 0

        lax.fori_loop(1, N, send_yw, 0)

    def local_q(h, _):
        acc_q[h] = tn(gl[h], yl[h])
        om, ow = om_ref[h], ow_ref[h]
        r = iota((1, BACK), 1)
        t = iota((T, BACK), 0)
        in_q = (r >= 64) & (r < 96)
        want_kv = jnp.where(r < 64, 4 * r + om, jnp.where((r >= 96) & (r < 100), 64 * (r - 96) + ow, -1))
        want_q = jnp.where(
            in_q, 4 * (r - 64) + om, jnp.where((r >= 100) & (r < 104), 64 * (r - 100) + ow, -1)
        )
        want_r = jnp.where(in_q, 4 * (r - 32) + om, -1)
        where_back[h, 0] = onehot(t == want_kv)
        where_back[h, 1] = onehot(t == want_q)
        where_back[h, 2] = onehot(t == want_r)
        return 0

    lax.fori_loop(0, HEADS, local_q, 0)

    @pl.when(active)
    def _():
        def get_keys(i, _):
            @pl.when(i != inner)
            def _():
                to_inner(msg_k.at[0], rx_k.at[i], mk_s.at[0], mk_r.at[i], i).wait_recv()

            y = rx_k[i]
            yk[i] = y * half_k
            yv[i] = y * half_v
            return 0

        lax.fori_loop(0, N, get_keys, 0)

        def get_st(i, _):
            @pl.when(i != inner)
            def _():
                to_inner(st_tx.at[0], st_rx.at[i], st_s.at[0], st_r.at[i], i).wait_recv()

            return 0

        lax.fori_loop(0, N, get_st, 0)

        om, ow = om_ref[head], ow_ref[head]
        even = head % 2 == 0

        def stat(index):
            return jnp.where(even, st_rx[:, index, :], st_rx[:, index + 4, :])

        def chunks(rows):
            ones = onehot(iota((8, N), 0) == (iota((8, N), 1) >> 1))
            a = rows.astype(BF).astype(F32)
            r = rows - a
            b = r.astype(BF).astype(F32)
            c = (r - b).astype(BF)
            return nn(ones, a.astype(BF)) + nn(ones, b.astype(BF)) + nn(ones, c)

        dm[...] = chunks(stat(0))
        lse_local_m = chunks(stat(1))
        delta_w = jnp.sum(stat(2), axis=0, keepdims=True)
        lse_local_w = jnp.sum(stat(3), axis=0, keepdims=True)

        def mid_a(u, _):
            b = (quad + 4 - u) % 4

            def get_queries(j, _):
                i = 4 * b + j

                @pl.when(i != inner)
                def _():
                    to_inner(msg_q.at[0], rx_q.at[i], mq_s.at[0], mq_r.at[i], i).wait_recv()

                return 0

            lax.fori_loop(0, 4, get_queries, 0)
            x = rx_q[pl.ds(4 * b, 4)].reshape(T, 128)
            delta = jnp.concatenate([dm[pl.ds(2 * b, 1), :], dm[pl.ds(2 * b + 1, 1), :]], axis=1)
            top = jnp.full((1, T), NEG, F32)
            for kb in range(4):
                s = nt(yk[4 * kb : 4 * kb + 4].reshape(T, 128), x)
                s_scr[kb] = s
                top = jnp.maximum(top, jnp.max(s, axis=0, keepdims=True))
            total = jnp.zeros((1, T), F32)
            dq = jnp.zeros((T, 128), F32)
            for kb in range(4):
                e = jnp.exp(s_scr[kb] - top)
                total = total + jnp.sum(e, axis=0, keepdims=True)
                d = nt(yv[4 * kb : 4 * kb + 4].reshape(T, 128), x)
                em[b, kb] = e.astype(BF)
                g = (e * (d - delta)).astype(BF)
                gm[b, kb] = g
                dq = dq + tn(g, rx_k[4 * kb : 4 * kb + 4].reshape(T, 128))
            dq_m[b] = dq
            lse = top + jnp.log(total)
            mm[pl.ds(2 * b, 1), :] = top[:, :128]
            mm[pl.ds(2 * b + 1, 1), :] = top[:, 128:]
            ml[pl.ds(2 * b, 1), :] = lse[:, :128]
            ml[pl.ds(2 * b + 1, 1), :] = lse[:, 128:]
            return 0

        lax.fori_loop(0, 4, mid_a, 0)

        def get_yw(i, _):
            @pl.when(i != outer)
            def _():
                to_outer(yw, rxo.at[i], yw_s.at[i], yw_r.at[i], i).wait_recv()

            return 0

        lax.fori_loop(0, N, get_yw, 0)

        all_y = rxo[...].reshape(N * 64, 128)
        x_w = xw_w[...]
        s = nt(all_y * half_k, x_w)
        top_w = jnp.max(s, axis=0, keepdims=True)
        e = jnp.exp(s - top_w)
        lse_w = top_w + jnp.log(jnp.sum(e, axis=0, keepdims=True))
        d = nt(all_y * half_v, x_w)
        ew = e.astype(BF)
        gw = (e * (d - delta_w[:, :64])).astype(BF)
        zeros64 = jnp.zeros((1, 64), F32)
        top_w = jnp.concatenate([top_w, zeros64], axis=1)
        lse_w = jnp.concatenate([lse_w, zeros64], axis=1)

        lse_m = ml[...]
        shared = (ow & 3) == om
        spot = jnp.where(shared, ow >> 2, -1)
        lane8, chunk8 = iota((8, 128), 1), iota((8, 128), 0)
        here = (lane8 & 15) == spot
        n128 = iota((128, 128), 1)
        spread = onehot(((n128 & 7) == (iota((128, 128), 0) >> 4)) & (n128 < 64))
        own = (lane8 >> 3) == chunk8
        m_at_w = sum3(nn(split3(jnp.where(here, lse_m, 0.0)), spread))
        m_at_w = jnp.sum(jnp.where(own, m_at_w, 0.0), axis=0, keepdims=True)
        w_at_m = sum3(nt(split3(jnp.where(own, lse_w, 0.0)), spread))
        total_m = lse3(lse_m, lse_local_m, jnp.where(here, w_at_m, NEG))
        spot_row = jnp.full((1, 128), spot, I32)
        total_w = lse3(lse_w, lse_local_w, jnp.where(spot_row >= 0, m_at_w, NEG))
        for j in range(8):
            ls_tx[j] = jnp.where(chunk8 == 0, lse_m[j : j + 1], lse_w)

        def send_ls(d, _):
            t = (inner + d) % N
            to_inner(ls_tx.at[t // 2], ls_rx.at[head], ls_s.at[t], ls_r.at[head], t).start()
            return 0

        lax.fori_loop(1, N, send_ls, 0)
        ls_rx[head] = ls_tx[inner // 2]

        weight_m = jnp.exp(mm[...] - total_m)
        weight_w = jnp.exp(top_w - total_w)
        stacked = jnp.concatenate(
            [weight_m, jnp.broadcast_to(weight_w, (8, 128)), jnp.zeros((112, 128), F32)], axis=0
        )
        columns = stacked.T

        col_w = columns[0:64, 8:9]
        scaled = (x_w.astype(F32) * col_w).astype(BF)
        wp[...] = jnp.where(left, nn(gw, scaled), nn(ew, scaled)).astype(BF).reshape(N, 64, 128)
        rxp[outer] = wp[outer]

        def send_wp(d, _):
            t = (outer + d) % N
            to_outer(wp.at[t], rxp.at[outer], wp_s.at[t], wp_r.at[outer], t).start()
            return 0

        lax.fori_loop(1, N, send_wp, 0)
        dq_w = (tn(gw, all_y) * col_w).astype(BF)

        for j in range(8):
            col = columns[:, j : j + 1]
            x = rx_q[2 * j : 2 * j + 2].reshape(128, 128).astype(F32)
            xw_all[128 * j : 128 * j + 128, :] = (x * col).astype(BF)
            dq = dq_m[j // 2, 128 * (j % 2) : 128 * (j % 2) + 128, :] * col
            for i in range(2):
                mine = dq[64 * i : 64 * i + 64]
                ret[2 * j + i, 64:96, :] = jnp.where(left, mine[:32], swap(mine[32:])).astype(BF)

        def send_rq(d, _):
            t = (inner + d) % N
            to_inner(
                ret.at[t, pl.ds(64, 32)], back.at[head, pl.ds(64, 32)], rq_s.at[t], rq_r.at[head], t
            ).start()
            return 0

        lax.fori_loop(1, N, send_rq, 0)

        def mid_b(u, _):
            kb = (quad + u) % 4
            from_g = jnp.zeros((T, 128), F32)
            from_e = jnp.zeros((T, 128), F32)
            for b in range(4):
                x = xw_all[256 * b : 256 * b + 256, :]
                from_g = from_g + nn(gm[b, kb], x)
                from_e = from_e + nn(em[b, kb], x)
            both = jnp.where(left, from_g, from_e).astype(BF)
            ret[pl.ds(4 * kb, 4), 0:64, :] = both.reshape(4, 64, 128)

            def send_rk(j, _):
                t = 4 * kb + (inner + j) % 4

                @pl.when(t != inner)
                def _():
                    to_inner(
                        ret.at[t, pl.ds(0, 64)], back.at[head, pl.ds(0, 64)], rk_s.at[t], rk_r.at[head], t
                    ).start()

                return 0

            lax.fori_loop(0, 4, send_rk, 0)
            return 0

        lax.fori_loop(0, 4, mid_b, 0)
        back[head, 0:96, :] = ret[inner]

        def get_wp(i, total):
            @pl.when(i != outer)
            def _():
                to_outer(wp.at[0], rxp.at[i], wp_s.at[0], wp_r.at[i], i).wait_recv()

            return total + rxp[i].astype(F32)

        kv_w = lax.fori_loop(0, N, get_wp, jnp.zeros((64, 128), F32)).astype(BF)
        r256, n64 = iota((T, 64), 0), iota((T, 64), 1)
        slot = r256 & 15
        at = 4 * (r256 >> 4) + (slot & 3)
        rows_w = nn(onehot((n64 == at) & (slot < 4)), kv_w)
        rows_w = rows_w + nn(onehot((n64 == at) & (slot >= 4) & (slot < 8)), dq_w)
        retw[...] = rows_w.astype(BF).reshape(N, 16, 128)

        def send_rw(d, _):
            t = (inner + d) % N
            to_inner(retw.at[t], back.at[head, pl.ds(96, 16)], rw_s.at[t], rw_r.at[head], t).start()
            return 0

        lax.fori_loop(1, N, send_rw, 0)
        back[head, 96:112, :] = retw[inner]

    def get_ls(h, _):
        t = device_of(h)

        @pl.when(t != inner)
        def _():
            to_inner(ls_tx.at[0], ls_rx.at[h], ls_s.at[0], ls_r.at[h], t).wait_recv()

        return 0

    lax.fori_loop(0, HEADS, get_ls, 0)

    def local_b(p, _):
        row = iota((8, 1), 0)
        first, second = ls_rx[2 * p], ls_rx[2 * p + 1]
        rows = jnp.where(
            row < 2,
            jnp.where(row == 0, first[0:1], second[0:1]),
            jnp.where(row == 2, first[1:2], second[1:2]),
        )
        parts = split3(rows)
        lse_m = sum3(nt(parts, place_m))[0:2]
        lse_w = sum3(nt(parts, place_w))[2:4]
        top, lse = mst[p][0:2], mst[p][2:4]
        row2 = iota((2, 1), 0)
        om = jnp.where(row2 == 0, om_ref[2 * p], om_ref[2 * p + 1])
        ow = jnp.where(row2 == 0, ow_ref[2 * p], ow_ref[2 * p + 1])
        total = lse3(
            lse, jnp.where((tok & 3) == om, lse_m, NEG), jnp.where((tok & 63) == ow, lse_w, NEG)
        )
        weight = jnp.exp(top - total)
        r128 = iota((128, 1), 0)
        columns = jnp.where(r128 == 0, weight[0:1], weight[1:2]).T
        for a in range(2):
            h = 2 * p + a
            col = columns[:, a : a + 1]
            x = (xl[h].astype(F32) * col).astype(BF)
            acc_kv[h] = jnp.where(left, nn(gl[h], x), nn(el[h], x))
            acc_q[h] = acc_q[h] * col
        return 0

    lax.fori_loop(0, HEADS // 2, local_b, 0)

    def get_back(h, _):
        t = device_of(h)

        @pl.when(t != inner)
        def _():
            to_inner(
                ret.at[0, pl.ds(64, 32)], back.at[h, pl.ds(64, 32)], rq_s.at[0], rq_r.at[h], t
            ).wait_recv()
            to_inner(
                ret.at[0, pl.ds(0, 64)], back.at[h, pl.ds(0, 64)], rk_s.at[0], rk_r.at[h], t
            ).wait_recv()
            to_inner(retw.at[0], back.at[h, pl.ds(96, 16)], rw_s.at[0], rw_r.at[h], t).wait_recv()
            to_inner(msg_w.at[h], rx_w.at[inner], mw_s.at[h], mw_r.at[inner], t).wait_send()
            to_inner(msg_k.at[h], rx_k.at[inner], mk_s.at[h], mk_r.at[inner], t).wait_send()
            to_inner(msg_q.at[h], rx_q.at[inner], mq_s.at[h], mq_r.at[inner], t).wait_send()
            to_inner(st_tx.at[h // 2], st_rx.at[inner], st_s.at[h], st_r.at[inner], t).wait_send()

        return 0

    lax.fori_loop(0, HEADS, get_back, 0)

    @pl.when(active)
    def _():
        def sent(d, _):
            t = (inner + d) % N
            to_inner(ls_tx.at[t // 2], ls_rx.at[head], ls_s.at[t], ls_r.at[head], t).wait_send()
            to_inner(
                ret.at[t, pl.ds(64, 32)], back.at[head, pl.ds(64, 32)], rq_s.at[t], rq_r.at[head], t
            ).wait_send()
            to_inner(
                ret.at[t, pl.ds(0, 64)], back.at[head, pl.ds(0, 64)], rk_s.at[t], rk_r.at[head], t
            ).wait_send()
            to_inner(retw.at[t], back.at[head, pl.ds(96, 16)], rw_s.at[t], rw_r.at[head], t).wait_send()
            t = (outer + d) % N
            to_outer(yw, rxo.at[outer], yw_s.at[t], yw_r.at[outer], t).wait_send()
            to_outer(wp.at[t], rxp.at[outer], wp_s.at[t], wp_r.at[outer], t).wait_send()
            return 0

        lax.fori_loop(1, N, sent, 0)


def finish(acc_kv, acc_q, back, where_back, dq_hbm, dk_hbm, dv_hbm, dq_ref, dk_ref, dv_ref, sems):
    left = iota((1, 128), 1) < 64
    copies = []
    for p in range(HEADS // 2):
        cols = pl.ds(p * 128, 128)
        kvs, qs, rest = [], [], []
        for a in range(2):
            h = 2 * p + a
            rows = back[h]
            kvs.append(acc_kv[h] + nn(where_back[h, 0], rows))
            qs.append(acc_q[h] + nn(where_back[h, 1], rows))
            rest.append(nn(where_back[h, 2], rows))
        dq = jnp.where(left, qs[0] + swap(rest[0]), swap(qs[1]) + rest[1])
        dq_ref[:, cols] = (SCALE * dq).astype(BF)
        dk_ref[:, cols] = (SCALE * jnp.where(left, kvs[0], swap(kvs[1]))).astype(BF)
        dv_ref[:, cols] = jnp.where(left, swap(kvs[0]), kvs[1]).astype(BF)
        if p % 2 == 1:
            wide = pl.ds((p - 1) * 128, 256)
            for i, (src, dst) in enumerate([(dq_ref, dq_hbm), (dk_ref, dk_hbm), (dv_ref, dv_hbm)]):
                copies.append(pltpu.make_async_copy(src.at[:, wide], dst.at[:, wide], sems.at[i, p // 2]))
                copies[-1].start()
    for copy in copies:
        copy.wait()


def per_device(queries, keys, values, saved_out, out_grad, offset_mid, offset_wide):
    vmem = pl.BlockSpec(memory_space=pltpu.VMEM)
    hbm = pl.BlockSpec(memory_space=pltpu.HBM)
    v = pltpu.VMEM
    dma = pltpu.SemaphoreType.DMA
    rows = jax.ShapeDtypeStruct((T, HEADS * 64), BF)
    parts = pl.pallas_call(
        kernel,
        out_shape=(
            jax.ShapeDtypeStruct((HEADS, T, 128), F32),
            jax.ShapeDtypeStruct((HEADS, T, 128), F32),
            jax.ShapeDtypeStruct((HEADS, BACK, 128), BF),
            jax.ShapeDtypeStruct((HEADS, 3, T, BACK), BF),
        ),
        in_specs=[hbm] * 7,
        out_specs=(vmem,) * 4,
        scratch_shapes=[
            pltpu.SMEM((HEADS,), I32),
            pltpu.SMEM((HEADS,), I32),
            v((T, HEADS * 64), BF),
            v((T, HEADS * 64), BF),
            v((T, HEADS * 64), BF),
            v((T, HEADS * 64), BF),
            v((T, HEADS * 64), BF),
            v((HEADS, T, 128), BF),
            v((HEADS, T, 128), BF),
            v((HEADS, 16, 128), BF),
            v((HEADS, 64, 128), BF),
            v((HEADS, 64, 128), BF),
            v((N, 16, 128), BF),
            v((N, 64, 128), BF),
            v((N, 64, 128), BF),
            v((HEADS, T, T), BF),
            v((HEADS, T, T), BF),
            v((HEADS // 2, 8, T), F32),
            v((HEADS // 2, 8, 128), F32),
            v((N, 8, 128), F32),
            v((8, 8, 128), F32),
            v((HEADS, 8, 128), F32),
            v((N, 64, 128), BF),
            v((N, 64, 128), BF),
            v((4, T, T), F32),
            v((4, 4, T, T), BF),
            v((4, 4, T, T), BF),
            v((8, 128), F32),
            v((8, 128), F32),
            v((8, 128), F32),
            v((4, T, 128), F32),
            v((N * 64, 128), BF),
            v((64, 128), BF),
            v((64, 128), BF),
            v((N, 64, 128), BF),
            v((N, 64, 128), BF),
            v((N, 64, 128), BF),
            v((N, 96, 128), BF),
            v((N, 16, 128), BF),
            dma((7,)),
            dma((HEADS,)), dma((N,)),
            dma((HEADS,)), dma((N,)),
            dma((HEADS,)), dma((N,)),
            dma((HEADS,)), dma((N,)),
            dma((N,)), dma((HEADS,)),
            dma((N,)), dma((N,)),
            dma((N,)), dma((N,)),
            dma((N,)), dma((HEADS,)),
            dma((N,)), dma((HEADS,)),
            dma((N,)), dma((HEADS,)),
        ],
        compiler_params=pltpu.CompilerParams(
            collective_id=0, has_side_effects=True, vmem_limit_bytes=40 * 1024 * 1024
        ),
    )(
        *[
            pltpu.with_memory_space_constraint(x, pltpu.HBM)
            for x in (offset_mid, offset_wide, queries, keys, values, saved_out, out_grad)
        ]
    )
    return pl.pallas_call(
        finish,
        out_shape=(rows, rows, rows),
        in_specs=[vmem] * 4,
        out_specs=(hbm,) * 3,
        scratch_shapes=[v((T, HEADS * 64), BF)] * 3 + [dma((3, 3))],
        compiler_params=pltpu.CompilerParams(vmem_limit_bytes=40 * 1024 * 1024),
    )(*parts)


def solution(mesh):
    rows = P(("outer", "inner"), None)
    return jax.shard_map(
        per_device,
        mesh=mesh,
        in_specs=(rows, rows, rows, rows, rows, P(), P()),
        out_specs=(rows, rows, rows),
        check_vma=False,
    )
```

```python
import jax
import jax.numpy as jnp
from jax import lax
from jax.experimental import pallas as pl
from jax.experimental.pallas import tpu as pltpu
from jax.sharding import PartitionSpec as P

BF = jnp.bfloat16
F32 = jnp.float32
I32 = jnp.int32

N = 16
HEADS = 12
T = 256
MID = 64
SCALE = 0.125
NEG = -1e30
BACK = 112


def iota(shape, dim):
    return lax.broadcasted_iota(I32, shape, dim)


def nn(a, b):
    return lax.dot_general(a, b, (((1,), (0,)), ((), ())), preferred_element_type=F32)


def nt(a, b):
    return lax.dot_general(a, b, (((1,), (1,)), ((), ())), preferred_element_type=F32)


def tn(a, b):
    return lax.dot_general(a, b, (((0,), (0,)), ((), ())), preferred_element_type=F32)


def onehot(mask):
    return jnp.where(mask, 1.0, 0.0).astype(BF)


def split3(x):
    a = x.astype(BF).astype(F32)
    r = x - a
    b = r.astype(BF).astype(F32)
    return jnp.concatenate([a, b, r - b], axis=0).astype(BF)


def sum3(x):
    r = x.shape[0] // 3
    return x[:r] + x[r : 2 * r] + x[2 * r :]


def lse3(a, b, c):
    top = jnp.maximum(a, jnp.maximum(b, c))
    return top + jnp.log(jnp.exp(a - top) + jnp.exp(b - top) + jnp.exp(c - top))


def swap(x):
    return pltpu.roll(x, 64, 1)


def kernel(
    om_hbm, ow_hbm, q_hbm, k_hbm, v_hbm, o_hbm, g_hbm,
    acc_kv, acc_q, back, where_back,
    om_ref, ow_ref, q_ref, k_ref, v_ref, o_ref, g_ref,
    xl, yl, msg_w, msg, rx_w, rx, el, gl, dl, top_l, sum_l, cols_l, st_tx, st_rx, ls_tx, ls_rx,
    yk, yv, s_scr, em, gm, mm, sm, dm, lm, wm, dq_m, xw_all, xw_w, yw, rxo, wp, rxp, ret, retw,
    in_s, mw_s, mw_r, m_s, m_r, st_s, st_r, ls_s, ls_r, yw_s, yw_r, wp_s, wp_r,
    rk_s, rk_r, rq_s, rq_r, rw_s, rw_r,
):
    inner = lax.axis_index("inner")
    outer = lax.axis_index("outer")
    quad = inner // 4
    active = inner % 4 < 3
    head = jnp.minimum(quad * 3 + inner % 4, HEADS - 1)

    def to_inner(src, dst, send, recv, target):
        return pltpu.make_async_remote_copy(
            src_ref=src, dst_ref=dst, send_sem=send, recv_sem=recv,
            device_id={"inner": target}, device_id_type=pl.DeviceIdType.MESH,
        )

    def to_outer(src, dst, send, recv, target):
        return pltpu.make_async_remote_copy(
            src_ref=src, dst_ref=dst, send_sem=send, recv_sem=recv,
            device_id={"outer": target}, device_id_type=pl.DeviceIdType.MESH,
        )

    loads = [
        pltpu.make_async_copy(src, dst, in_s.at[i])
        for i, (src, dst) in enumerate(
            [
                (om_hbm, om_ref), (ow_hbm, ow_ref), (q_hbm, q_ref), (g_hbm, g_ref),
                (k_hbm, k_ref), (v_hbm, v_ref), (o_hbm, o_ref),
            ]
        )
    ]
    for load in loads:
        load.start()

    barrier = pltpu.get_barrier_semaphore()

    def greet(d, _):
        pl.semaphore_signal(
            barrier, inc=1, device_id={"inner": (inner + d) % N}, device_id_type=pl.DeviceIdType.MESH
        )
        pl.semaphore_signal(
            barrier, inc=1, device_id={"outer": (outer + d) % N}, device_id_type=pl.DeviceIdType.MESH
        )
        return 0

    lax.fori_loop(1, N, greet, 0)
    for load in loads:
        load.wait()

    left = iota((1, 128), 1) < 64
    half_k = jnp.where(left, SCALE, 0.0).astype(BF)
    half_v = jnp.where(left, 0.0, 1.0).astype(BF)

    def block_of(u):
        return (quad // 2 + 1 - u // 2) % 2 * 2 + (quad + 1 - u % 2) % 2

    t_row = iota((T, 128), 0)
    t_lane = iota((T, 128), 1)
    place_m = onehot(t_lane == (t_row >> 2) + 64 * (inner % 2))
    place_w = onehot(t_lane == (t_row >> 6) + 4 * inner)
    tok = iota((1, T), 1)
    head_row = iota((16, 1), 0)
    om_col, ow_col = jnp.zeros((16, 1), I32), jnp.zeros((16, 1), I32)
    for h in range(HEADS):
        om_col = jnp.where(head_row == h, om_ref[h], om_col)
        ow_col = jnp.where(head_row == h, ow_ref[h], ow_col)
    keep_m = (tok & 3) == om_col
    keep_w = (tok & 63) == ow_col

    prod = g_ref[...].astype(F32) * o_ref[...].astype(F32)
    hi = prod.astype(BF)
    lo = (prod - hi.astype(F32)).astype(BF)
    of_head = onehot(iota((16, HEADS * 64), 0) == (iota((16, HEADS * 64), 1) >> 6))
    delta = nt(of_head, hi) + nt(of_head, lo)
    dl[...] = delta
    delta_m = nn(split3(jnp.where(keep_m, delta, 0.0)), place_m)
    delta_w = nn(split3(jnp.where(keep_w, delta, 0.0)), place_w)

    row16 = iota((16, 1), 0)
    for p in range(HEADS // 2):
        cols = pl.ds(p * 128, 128)
        qp, kp, vp, gp = q_ref[:, cols], k_ref[:, cols], v_ref[:, cols], g_ref[:, cols]
        for a in range(2):
            h = 2 * p + a
            b, c = 64 * a, 64 * a + 64
            x = jnp.concatenate([qp[:, b:c], gp[:, b:c]], axis=1)
            y = jnp.concatenate([kp[:, b:c], vp[:, b:c]], axis=1)
            xl[h] = x
            yl[h] = y
            om, ow = om_ref[h], ow_ref[h]
            row = iota((96, 1), 0)
            r = row - 64
            w = r & 15
            wide = jnp.where((r < 16) & (w < 4), 64 * w + ow, -1)
            wide = jnp.where((r >= 16) & (w >= 4) & (w < 8), 64 * (w - 4) + ow, wide)
            want = jnp.where(row < 64, 4 * row + om, wide)
            pick = onehot(iota((96, T), 1) == want)
            got = nn(pick, jnp.concatenate([x, y], axis=1))
            msg[h, 0:64, :] = got[0:64, 128:256].astype(BF)
            msg[h, 64:128, :] = got[0:64, 0:128].astype(BF)
            tile = got[64:80, 0:128] + got[80:96, 128:256]
            for i in range(3):
                tile = jnp.where(row16 == 8 + i, delta_m[16 * i + h : 16 * i + h + 1], tile)
                tile = jnp.where(row16 == 11 + i, delta_w[16 * i + h : 16 * i + h + 1], tile)
            msg_w[h] = tile.astype(BF)
    pl.semaphore_wait(barrier, 2 * (N - 1))

    def block_of(u):
        return (quad // 2 + 1 - u // 2) % 2 * 2 + (quad + 1 - u % 2) % 2

    def send_to_heads(src_of, dst, send, recv):
        for i in range(HEADS):
            block = block_of(i // 3)
            j = (i + inner) % 3
            h, target = 3 * block + j, 4 * block + j
            if i < 9:
                to_inner(src_of(h), dst.at[inner], send, recv, target).start()
            else:

                @pl.when(target != inner)
                def _():
                    to_inner(src_of(h), dst.at[inner], send, recv, target).start()

    def got_inner(dst, recv):
        to_inner(dst, dst, recv, recv, (inner + 1) % N).wait_recv()

    def got_outer(dst, recv):
        to_outer(dst, dst, recv, recv, (outer + 1) % N).wait_recv()

    def sent_inner(src, send):
        to_inner(src, src, send, send, (inner + 1) % N).wait_send()

    def sent_outer(src, send):
        to_outer(src, src, send, send, (outer + 1) % N).wait_send()

    send_to_heads(lambda h: msg_w.at[h], rx_w, mw_s, mw_r)
    send_to_heads(lambda h: msg.at[h], rx, m_s, m_r)

    @pl.when(active)
    def _():
        rx_w[inner] = msg_w[head]
        rx[inner] = msg[head]

    top_l[...] = jnp.zeros((16, T), F32)
    sum_l[...] = jnp.ones((16, T), F32)

    def local_a(h, _):
        x, y = xl[h], yl[h]
        s = nt(y * half_k, x)
        top = jnp.max(s, axis=0, keepdims=True)
        e = jnp.exp(s - top)
        top_l[pl.ds(h, 1), :] = top
        sum_l[pl.ds(h, 1), :] = jnp.sum(e, axis=0, keepdims=True)
        d = nt(y * half_v, x)
        el[h] = e.astype(BF)
        gl[h] = (e * (d - dl[pl.ds(h, 1), :])).astype(BF)
        return 0

    lax.fori_loop(0, HEADS, local_a, 0, unroll=3)
    @pl.when(active)
    def _():
        got_inner(rx_w.at[pl.ds(0, N - 1)], mw_r)
        r, c = iota((144, T), 0), iota((144, T), 1)
        slot, owner = c & 15, c >> 4
        at = 16 * ((r & 63) >> 2) + (r & 3)
        j = r - 128
        take = jnp.where(r < 64, jnp.where(c == at, 1, 0), jnp.where(c == at + 4, 1, 0))
        in_m = jnp.where((slot >= 8) & (slot < 11) & ((owner >> 1) == j), 1, 0)
        in_w = jnp.where((slot >= 11) & (slot < 14) & (j == 8), 1, 0)
        take = jnp.where(r < 128, take, in_m + in_w)
        got = nn(onehot(take > 0), rx_w[...].reshape(T, 128))
        xw_w[...] = got[0:64].astype(BF)
        yw[...] = got[64:128].astype(BF)
        dm[...] = got[128:144]
        rxo[outer] = yw[...]
        for d in range(1, N):
            t = (outer + d) % N
            to_outer(yw, rxo.at[outer], yw_s, yw_r, t).start()

    lse_l = top_l[...] + jnp.log(sum_l[...])
    lse_m = sum3(nn(split3(jnp.where(keep_m, lse_l, 0.0)), place_m))
    lse_w = sum3(nn(split3(jnp.where(keep_w, lse_l, 0.0)), place_w))
    row8 = iota((8, 1), 0)
    for h in range(HEADS):
        st_tx[h] = jnp.where(row8 == 0, lse_m[h : h + 1], lse_w[h : h + 1])
    send_to_heads(lambda h: st_tx.at[h], st_rx, st_s, st_r)

    @pl.when(active)
    def _():
        st_rx[inner] = st_tx[head]

    def local_q(h, _):
        acc_q[h] = tn(gl[h], yl[h])
        om, ow = om_ref[h], ow_ref[h]
        r = iota((1, BACK), 1)
        t = iota((T, BACK), 0)
        in_q = (r >= 64) & (r < 96)
        want_kv = jnp.where(r < 64, 4 * r + om, jnp.where((r >= 96) & (r < 100), 64 * (r - 96) + ow, -1))
        want_q = jnp.where(
            in_q, 4 * (r - 64) + om, jnp.where((r >= 100) & (r < 104), 64 * (r - 100) + ow, -1)
        )
        want_r = jnp.where(in_q, 4 * (r - 32) + om, -1)
        where_back[h, 0] = onehot(t == want_kv)
        where_back[h, 1] = onehot(t == want_q)
        where_back[h, 2] = onehot(t == want_r)
        return 0

    lax.fori_loop(0, HEADS, local_q, 0, unroll=3)

    @pl.when(active)
    def _():
        got_inner(rx.at[pl.ds(0, N - 1)], m_r)
        om, ow = om_ref[head], ow_ref[head]
        yk[...] = rx[:, 0:64, :] * half_k
        yv[...] = rx[:, 0:64, :] * half_v

        def mid_a(b):
            x = rx[4 * b : 4 * b + 4, 64:128, :].reshape(T, 128)
            delta = jnp.concatenate([dm[2 * b : 2 * b + 1, :], dm[2 * b + 1 : 2 * b + 2, :]], axis=1)
            top = jnp.full((1, T), NEG, F32)
            for kb in range(4):
                s = nt(yk[4 * kb : 4 * kb + 4].reshape(T, 128), x)
                s_scr[b, kb] = s
                top = jnp.maximum(top, jnp.max(s, axis=0, keepdims=True))
            total = jnp.zeros((1, T), F32)
            dq = jnp.zeros((T, 128), F32)
            for kb in range(4):
                e = jnp.exp(s_scr[b, kb] - top)
                total = total + jnp.sum(e, axis=0, keepdims=True)
                d = nt(yv[4 * kb : 4 * kb + 4].reshape(T, 128), x)
                em[b, kb] = e.astype(BF)
                g = (e * (d - delta)).astype(BF)
                gm[b, kb] = g
                dq = dq + tn(g, rx[4 * kb : 4 * kb + 4, 0:64, :].reshape(T, 128))
            dq_m[b] = dq
            for i in range(2):
                mm[2 * b + i : 2 * b + i + 1, :] = top[:, 128 * i : 128 * i + 128]
                sm[2 * b + i : 2 * b + i + 1, :] = total[:, 128 * i : 128 * i + 128]

        for b in range(4):
            mid_a(b)

        got_inner(st_rx.at[pl.ds(0, N - 1)], st_r)
        ones = onehot(iota((8, N), 0) == (iota((8, N), 1) >> 1))
        rows = st_rx[:, 0, :]
        first = rows.astype(BF).astype(F32)
        second = (rows - first).astype(BF).astype(F32)
        third = rows - first - second
        lm[...] = nn(ones, first.astype(BF)) + nn(ones, second.astype(BF)) + nn(ones, third.astype(BF))
        lse_local_w = jnp.sum(st_rx[:, 1, :], axis=0, keepdims=True)
        got_outer(rxo.at[pl.ds(0, N - 1)], yw_r)

        all_y = rxo[...].reshape(N * 64, 128)
        x_w = xw_w[...]
        s = nt(all_y * half_k, x_w)
        top_w = jnp.max(s, axis=0, keepdims=True)
        e = jnp.exp(s - top_w)
        lse_w = top_w + jnp.log(jnp.sum(e, axis=0, keepdims=True))
        d = nt(all_y * half_v, x_w)
        ew = e.astype(BF)
        gw = (e * (d - dm[8:9, 0:64])).astype(BF)
        s = nt(yk[...].reshape(N * 64, 128), x_w)
        top = jnp.max(s, axis=0, keepdims=True)
        m_at_w = top + jnp.log(jnp.sum(jnp.exp(s - top), axis=0, keepdims=True))
        shared = (ow & 3) == om
        spot = jnp.where(shared, ow >> 2, -1)
        spot_row = jnp.full((1, 64), spot, I32)
        total_w = lse3(lse_w, lse_local_w[:, :64], jnp.where(spot_row >= 0, m_at_w, NEG))
        weight_w = jnp.exp(top_w - total_w)
        zeros64 = jnp.zeros((1, 64), F32)
        col_w = jnp.broadcast_to(jnp.concatenate([weight_w, zeros64], axis=1), (128, 128)).T[0:64, 0:1]
        scaled = (x_w.astype(F32) * col_w).astype(BF)
        wp[...] = jnp.where(left, nn(gw, scaled), nn(ew, scaled)).astype(BF).reshape(N, 64, 128)
        rxp[outer] = wp[outer]

        for d in range(1, N):
            t = (outer + d) % N
            to_outer(wp.at[t], rxp.at[outer], wp_s, wp_r, t).start()

        dq_w = (tn(gw, all_y) * col_w).astype(BF)

        lse_w = jnp.concatenate([lse_w, zeros64], axis=1)
        lane8, chunk8 = iota((8, 128), 1), iota((8, 128), 0)
        n128 = iota((128, 128), 1)
        spread = onehot(((n128 & 7) == (iota((128, 128), 0) >> 4)) & (n128 < 64))
        w_at_m = sum3(nt(split3(jnp.where((lane8 >> 3) == chunk8, lse_w, 0.0)), spread))
        wm[...] = jnp.where((lane8 & 15) == spot, w_at_m, NEG)

        for b in range(4, 4):
            mid_a(b)
        lse_m = mm[...] + jnp.log(sm[...])
        weight_m = jnp.exp(mm[...] - lse3(lse_m, lm[...], wm[...]))
        columns = jnp.concatenate([weight_m, jnp.zeros((120, 128), F32)], axis=0).T
        for j in range(8):
            ls_tx[j] = jnp.where(chunk8 == 0, lse_m[j : j + 1], lse_w)
            col = columns[:, j : j + 1]
            x = rx[2 * j : 2 * j + 2, 64:128, :].reshape(128, 128).astype(F32)
            xw_all[j // 2, 128 * (j % 2) : 128 * (j % 2) + 128, :] = (x * col).astype(BF)
            dq = dq_m[j // 2, 128 * (j % 2) : 128 * (j % 2) + 128, :] * col
            for i in range(2):
                mine = dq[64 * i : 64 * i + 64]
                ret[2 * j + i, 64:96, :] = jnp.where(left, mine[:32], swap(mine[32:])).astype(BF)
        for d in range(1, N):
            t = (inner + d) % N
            to_inner(ls_tx.at[t // 2], ls_rx.at[head], ls_s, ls_r, t).start()
        for d in range(1, N):
            t = (inner + d) % N
            to_inner(ret.at[t, pl.ds(64, 32)], back.at[head, pl.ds(64, 32)], rq_s, rq_r, t).start()
        ls_rx[head] = ls_tx[inner // 2]

        def mid_b(u, _):
            kb = block_of(u)
            from_g = jnp.zeros((T, 128), F32)
            from_e = jnp.zeros((T, 128), F32)
            for b in range(4):
                x = xw_all[b]
                from_g = from_g + nn(gm[b, kb], x)
                from_e = from_e + nn(em[b, kb], x)
            both = jnp.where(left, from_g, from_e).astype(BF)
            ret[pl.ds(4 * kb, 4), 0:64, :] = both.reshape(4, 64, 128)

            for j in range(4):
                t = 4 * kb + (inner + j) % 4

                @pl.when(t != inner)
                def _():
                    to_inner(ret.at[t, pl.ds(0, 64)], back.at[head, pl.ds(0, 64)], rk_s, rk_r, t).start()

            return 0

        lax.fori_loop(0, 4, mid_b, 0)
        back[head, 0:96, :] = ret[inner]

        got_outer(rxp.at[pl.ds(0, N - 1)], wp_r)
        kv_w = jnp.sum(rxp[...].astype(F32), axis=0).astype(BF)
        r256, n64 = iota((T, 64), 0), iota((T, 64), 1)
        slot = r256 & 15
        at = 4 * (r256 >> 4) + (slot & 3)
        rows_w = nn(onehot((n64 == at) & (slot < 4)), kv_w)
        rows_w = rows_w + nn(onehot((n64 == at) & (slot >= 4) & (slot < 8)), dq_w)
        retw[...] = rows_w.astype(BF).reshape(N, 16, 128)

        for d in range(1, N):
            t = (inner + d) % N
            to_inner(retw.at[t], back.at[head, pl.ds(96, 16)], rw_s, rw_r, t).start()
        back[head, 96:112, :] = retw[inner]

    @pl.when(active)
    def _():
        got_inner(ls_rx.at[pl.ds(0, HEADS - 1)], ls_r)

    @pl.when(jnp.logical_not(active))
    def _():
        got_inner(ls_rx, ls_r)

    pad = jnp.zeros((4, 128), F32)
    lse_m = sum3(nt(split3(jnp.concatenate([ls_rx[:, 0, :], pad], axis=0)), place_m))
    lse_w = sum3(nt(split3(jnp.concatenate([ls_rx[:, 1, :], pad], axis=0)), place_w))
    total = lse3(lse_l, jnp.where(keep_m, lse_m, NEG), jnp.where(keep_w, lse_w, NEG))
    weight = jnp.exp(top_l[...] - total)
    cols_l[...] = jnp.concatenate([weight, jnp.zeros((112, T), F32)], axis=0).T
    for h in range(HEADS):
        col = cols_l[:, h : h + 1]
        x = (xl[h].astype(F32) * col).astype(BF)
        acc_kv[h] = jnp.where(left, nn(gl[h], x), nn(el[h], x))
        acc_q[h] = acc_q[h] * col

    def close(heads):
        got_inner(back.at[pl.ds(0, heads), pl.ds(64, 32)], rq_r)
        got_inner(back.at[pl.ds(0, heads), pl.ds(0, 64)], rk_r)
        got_inner(back.at[pl.ds(0, heads), pl.ds(96, 16)], rw_r)
        sent_inner(msg_w.at[pl.ds(0, heads)], mw_s)
        sent_inner(msg.at[pl.ds(0, heads)], m_s)
        sent_inner(st_rx.at[pl.ds(0, heads)], st_s)

    @pl.when(active)
    def _():
        close(HEADS - 1)
        sent_inner(st_rx.at[pl.ds(0, N - 1)], ls_s)
        sent_inner(ret.at[pl.ds(0, N - 1), pl.ds(64, 32)], rq_s)
        sent_inner(ret.at[pl.ds(0, N - 1), pl.ds(0, 64)], rk_s)
        sent_inner(retw.at[pl.ds(0, N - 1)], rw_s)
        sent_outer(rxo.at[pl.ds(0, N - 1)], yw_s)
        sent_outer(wp.at[pl.ds(0, N - 1)], wp_s)

    @pl.when(jnp.logical_not(active))
    def _():
        close(HEADS)


def finish(acc_kv, acc_q, back, where_back, dq_hbm, dk_hbm, dv_hbm, dq_ref, dk_ref, dv_ref, sems):
    left = iota((1, 128), 1) < 64
    copies = []
    for p in range(HEADS // 2):
        cols = pl.ds(p * 128, 128)
        kvs, qs, rest = [], [], []
        for a in range(2):
            h = 2 * p + a
            rows = back[h]
            kvs.append(acc_kv[h] + nn(where_back[h, 0], rows))
            qs.append(acc_q[h] + nn(where_back[h, 1], rows))
            rest.append(nn(where_back[h, 2], rows))
        dq = jnp.where(left, qs[0] + swap(rest[0]), swap(qs[1]) + rest[1])
        dq_ref[:, cols] = (SCALE * dq).astype(BF)
        dk_ref[:, cols] = (SCALE * jnp.where(left, kvs[0], swap(kvs[1]))).astype(BF)
        dv_ref[:, cols] = jnp.where(left, swap(kvs[0]), kvs[1]).astype(BF)
        if p % 2 == 1:
            wide = pl.ds((p - 1) * 128, 256)
            for i, (src, dst) in enumerate([(dq_ref, dq_hbm), (dk_ref, dk_hbm), (dv_ref, dv_hbm)]):
                copies.append(pltpu.make_async_copy(src.at[:, wide], dst.at[:, wide], sems.at[i, p // 2]))
                copies[-1].start()
    for copy in copies:
        copy.wait()


def per_device(queries, keys, values, saved_out, out_grad, offset_mid, offset_wide):
    vmem = pl.BlockSpec(memory_space=pltpu.VMEM)
    hbm = pl.BlockSpec(memory_space=pltpu.HBM)
    v = pltpu.VMEM
    dma = pltpu.SemaphoreType.DMA
    rows = jax.ShapeDtypeStruct((T, HEADS * 64), BF)
    parts = pl.pallas_call(
        kernel,
        out_shape=(
            jax.ShapeDtypeStruct((HEADS, T, 128), F32),
            jax.ShapeDtypeStruct((HEADS, T, 128), F32),
            jax.ShapeDtypeStruct((HEADS, BACK, 128), BF),
            jax.ShapeDtypeStruct((HEADS, 3, T, BACK), BF),
        ),
        in_specs=[hbm] * 7,
        out_specs=(vmem,) * 4,
        scratch_shapes=[
            pltpu.SMEM((HEADS,), I32),
            pltpu.SMEM((HEADS,), I32),
            v((T, HEADS * 64), BF),
            v((T, HEADS * 64), BF),
            v((T, HEADS * 64), BF),
            v((T, HEADS * 64), BF),
            v((T, HEADS * 64), BF),
            v((HEADS, T, 128), BF),
            v((HEADS, T, 128), BF),
            v((HEADS, 16, 128), BF),
            v((HEADS, 128, 128), BF),
            v((N, 16, 128), BF),
            v((N, 128, 128), BF),
            v((HEADS, T, T), BF),
            v((HEADS, T, T), BF),
            v((16, T), F32),
            v((16, T), F32),
            v((16, T), F32),
            v((T, 128), F32),
            v((HEADS, 8, 128), F32),
            v((N, 8, 128), F32),
            v((8, 8, 128), F32),
            v((HEADS, 8, 128), F32),
            v((N, 64, 128), BF),
            v((N, 64, 128), BF),
            v((4, 4, T, T), F32),
            v((4, 4, T, T), BF),
            v((4, 4, T, T), BF),
            v((8, 128), F32),
            v((8, 128), F32),
            v((16, 128), F32),
            v((8, 128), F32),
            v((8, 128), F32),
            v((4, T, 128), F32),
            v((4, T, 128), BF),
            v((64, 128), BF),
            v((64, 128), BF),
            v((N, 64, 128), BF),
            v((N, 64, 128), BF),
            v((N, 64, 128), BF),
            v((N, 96, 128), BF),
            v((N, 16, 128), BF),
            dma((7,)),
            dma, dma,
            dma, dma,
            dma, dma,
            dma, dma,
            dma, dma,
            dma, dma,
            dma, dma,
            dma, dma,
            dma, dma,
        ],
        compiler_params=pltpu.CompilerParams(
            collective_id=0, has_side_effects=True, vmem_limit_bytes=44 * 1024 * 1024
        ),
    )(
        *[
            pltpu.with_memory_space_constraint(x, pltpu.HBM)
            for x in (offset_mid, offset_wide, queries, keys, values, saved_out, out_grad)
        ]
    )
    return pl.pallas_call(
        finish,
        out_shape=(rows, rows, rows),
        in_specs=[vmem] * 4,
        out_specs=(hbm,) * 3,
        scratch_shapes=[v((T, HEADS * 64), BF)] * 3 + [dma((3, 3))],
        compiler_params=pltpu.CompilerParams(vmem_limit_bytes=40 * 1024 * 1024),
    )(*parts)


def solution(mesh):
    rows = P(("outer", "inner"), None)
    return jax.shard_map(
        per_device,
        mesh=mesh,
        in_specs=(rows, rows, rows, rows, rows, P(), P()),
        out_specs=(rows, rows, rows),
        check_vma=False,
    )
```

```python
import jax
import jax.numpy as jnp
from jax import lax
from jax.experimental import pallas as pl
from jax.experimental.pallas import tpu as pltpu
from jax.sharding import PartitionSpec as P

BF = jnp.bfloat16
F32 = jnp.float32
I32 = jnp.int32

N = 16
HEADS = 12
T = 256
MID = 64
SCALE = 0.125
NEG = -1e30
BACK = 112


def iota(shape, dim):
    return lax.broadcasted_iota(I32, shape, dim)


def nn(a, b):
    return lax.dot_general(a, b, (((1,), (0,)), ((), ())), preferred_element_type=F32)


def nt(a, b):
    return lax.dot_general(a, b, (((1,), (1,)), ((), ())), preferred_element_type=F32)


def tn(a, b):
    return lax.dot_general(a, b, (((0,), (0,)), ((), ())), preferred_element_type=F32)


def onehot(mask):
    return jnp.where(mask, 1.0, 0.0).astype(BF)


def split3(x):
    a = x.astype(BF).astype(F32)
    r = x - a
    b = r.astype(BF).astype(F32)
    return jnp.concatenate([a, b, r - b], axis=0).astype(BF)


def sum3(x):
    r = x.shape[0] // 3
    return x[:r] + x[r : 2 * r] + x[2 * r :]


def lse3(a, b, c):
    top = jnp.maximum(a, jnp.maximum(b, c))
    return top + jnp.log(jnp.exp(a - top) + jnp.exp(b - top) + jnp.exp(c - top))


def swap(x):
    return pltpu.roll(x, 64, 1)


def kernel(
    om_hbm, ow_hbm, q_hbm, k_hbm, v_hbm, o_hbm, g_hbm,
    acc_kv, acc_q, back, where_back,
    om_ref, ow_ref, q_ref, k_ref, v_ref, o_ref, g_ref,
    xl, yl, msg_w, msg, rx_w, rx, el, gl, dl, top_l, sum_l, cols_l, st_tx, st_rx, ls_tx, ls_rx,
    yk, yv, s_scr, em, gm, mm, sm, dm, lm, wm, xw_all, xw_w, yw, rxo, wp, rxp, ret, retw,
    in_s, mw_s, mw_r, mk_s, mk_r, mq_s, mq_r, st_s, st_r, ls_s, ls_r, yw_s, yw_r, wp_s, wp_r,
    rk_s, rk_r, rq_s, rq_r, rw_s, rw_r,
):
    inner = lax.axis_index("inner")
    outer = lax.axis_index("outer")
    quad = inner // 4
    active = inner % 4 < 3
    head = jnp.minimum(quad * 3 + inner % 4, HEADS - 1)

    def to_inner(src, dst, send, recv, target):
        return pltpu.make_async_remote_copy(
            src_ref=src, dst_ref=dst, send_sem=send, recv_sem=recv,
            device_id={"inner": target}, device_id_type=pl.DeviceIdType.MESH,
        )

    def to_outer(src, dst, send, recv, target):
        return pltpu.make_async_remote_copy(
            src_ref=src, dst_ref=dst, send_sem=send, recv_sem=recv,
            device_id={"outer": target}, device_id_type=pl.DeviceIdType.MESH,
        )

    loads = [
        pltpu.make_async_copy(src, dst, in_s.at[i])
        for i, (src, dst) in enumerate(
            [
                (om_hbm, om_ref), (ow_hbm, ow_ref), (q_hbm, q_ref), (g_hbm, g_ref),
                (k_hbm, k_ref), (v_hbm, v_ref), (o_hbm, o_ref),
            ]
        )
    ]
    barrier = pltpu.get_barrier_semaphore()

    for load in loads:
        load.start()

    def greet(d, _):
        pl.semaphore_signal(
            barrier, inc=1, device_id={"inner": (inner + d) % N}, device_id_type=pl.DeviceIdType.MESH
        )
        pl.semaphore_signal(
            barrier, inc=1, device_id={"outer": (outer + d) % N}, device_id_type=pl.DeviceIdType.MESH
        )
        return 0

    lax.fori_loop(1, N, greet, 0)
    for load in loads:
        load.wait()

    left = iota((1, 128), 1) < 64
    half_k = jnp.where(left, SCALE, 0.0).astype(BF)
    half_v = jnp.where(left, 0.0, 1.0).astype(BF)

    def block_of(u):
        return (quad // 2 + 1 - u // 2) % 2 * 2 + (quad + 1 - u % 2) % 2

    t_row = iota((T, 128), 0)
    t_lane = iota((T, 128), 1)
    place_m = onehot(t_lane == (t_row >> 2) + 64 * (inner % 2))
    place_w = onehot(t_lane == (t_row >> 6) + 4 * inner)
    tok = iota((1, T), 1)
    head_row = iota((16, 1), 0)
    om_col, ow_col = jnp.zeros((16, 1), I32), jnp.zeros((16, 1), I32)
    for h in range(HEADS):
        om_col = jnp.where(head_row == h, om_ref[h], om_col)
        ow_col = jnp.where(head_row == h, ow_ref[h], ow_col)
    keep_m = (tok & 3) == om_col
    keep_w = (tok & 63) == ow_col

    prod = g_ref[...].astype(F32) * o_ref[...].astype(F32)
    hi = prod.astype(BF)
    lo = (prod - hi.astype(F32)).astype(BF)
    of_head = onehot(iota((16, HEADS * 64), 0) == (iota((16, HEADS * 64), 1) >> 6))
    delta = nt(of_head, hi) + nt(of_head, lo)
    dl[...] = delta
    delta_m = nn(split3(jnp.where(keep_m, delta, 0.0)), place_m)
    delta_w = nn(split3(jnp.where(keep_w, delta, 0.0)), place_w)

    row16 = iota((16, 1), 0)
    for p in range(HEADS // 2):
        cols = pl.ds(p * 128, 128)
        qp, kp, vp, gp = q_ref[:, cols], k_ref[:, cols], v_ref[:, cols], g_ref[:, cols]
        for a in range(2):
            h = 2 * p + a
            b, c = 64 * a, 64 * a + 64
            x = jnp.concatenate([qp[:, b:c], gp[:, b:c]], axis=1)
            y = jnp.concatenate([kp[:, b:c], vp[:, b:c]], axis=1)
            xl[h] = x
            yl[h] = y
            om, ow = om_ref[h], ow_ref[h]
            row = iota((96, 1), 0)
            r = row - 64
            w = r & 15
            wide = jnp.where((r < 16) & (w < 4), 64 * w + ow, -1)
            wide = jnp.where((r >= 16) & (w >= 4) & (w < 8), 64 * (w - 4) + ow, wide)
            want = jnp.where(row < 64, 4 * row + om, wide)
            pick = onehot(iota((96, T), 1) == want)
            got = nn(pick, jnp.concatenate([x, y], axis=1))
            msg[h, 0:64, :] = got[0:64, 128:256].astype(BF)
            msg[h, 64:128, :] = got[0:64, 0:128].astype(BF)
            tile = got[64:80, 0:128] + got[80:96, 128:256]
            for i in range(3):
                tile = jnp.where(row16 == 8 + i, delta_m[16 * i + h : 16 * i + h + 1], tile)
                tile = jnp.where(row16 == 11 + i, delta_w[16 * i + h : 16 * i + h + 1], tile)
            msg_w[h] = tile.astype(BF)
    pl.semaphore_wait(barrier, 2 * (N - 1))

    def block_of(u):
        return (quad // 2 + 1 - u // 2) % 2 * 2 + (quad + 1 - u % 2) % 2

    def send_to_heads(src_of, dst, send, recv, rows=None):
        place = dst.at[inner] if rows is None else dst.at[inner, rows]
        for i in range(HEADS):
            block = block_of(i // 3)
            j = (i + inner) % 3
            h, target = 3 * block + j, 4 * block + j
            if i < 9:
                to_inner(src_of(h), place, send, recv, target).start()
            else:

                @pl.when(target != inner)
                def _():
                    to_inner(src_of(h), place, send, recv, target).start()

    def got_inner(dst, recv):
        to_inner(dst, dst, recv, recv, (inner + 1) % N).wait_recv()

    def got_outer(dst, recv):
        to_outer(dst, dst, recv, recv, (outer + 1) % N).wait_recv()

    def sent_inner(src, send):
        to_inner(src, src, send, send, (inner + 1) % N).wait_send()

    def sent_outer(src, send):
        to_outer(src, src, send, send, (outer + 1) % N).wait_send()

    send_to_heads(lambda h: msg_w.at[h], rx_w, mw_s, mw_r)
    send_to_heads(lambda h: msg.at[h, pl.ds(0, 64)], rx, mk_s, mk_r, pl.ds(0, 64))
    send_to_heads(lambda h: msg.at[h, pl.ds(64, 64)], rx, mq_s, mq_r.at[quad], pl.ds(64, 64))

    @pl.when(active)
    def _():
        rx_w[inner] = msg_w[head]
        rx[inner] = msg[head]

    top_l[...] = jnp.zeros((16, T), F32)
    sum_l[...] = jnp.ones((16, T), F32)

    def local_a(h, _):
        x, y = xl[h], yl[h]
        s = nt(y * half_k, x)
        top = jnp.max(s, axis=0, keepdims=True)
        e = jnp.exp(s - top)
        top_l[pl.ds(h, 1), :] = top
        sum_l[pl.ds(h, 1), :] = jnp.sum(e, axis=0, keepdims=True)
        d = nt(y * half_v, x)
        el[h] = e.astype(BF)
        gl[h] = (e * (d - dl[pl.ds(h, 1), :])).astype(BF)
        return 0

    lax.fori_loop(0, HEADS, local_a, 0, unroll=3)
    @pl.when(active)
    def _():
        got_inner(rx_w.at[pl.ds(0, N - 1)], mw_r)
        r, c = iota((144, T), 0), iota((144, T), 1)
        slot, owner = c & 15, c >> 4
        at = 16 * ((r & 63) >> 2) + (r & 3)
        j = r - 128
        take = jnp.where(r < 64, jnp.where(c == at, 1, 0), jnp.where(c == at + 4, 1, 0))
        in_m = jnp.where((slot >= 8) & (slot < 11) & ((owner >> 1) == j), 1, 0)
        in_w = jnp.where((slot >= 11) & (slot < 14) & (j == 8), 1, 0)
        take = jnp.where(r < 128, take, in_m + in_w)
        got = nn(onehot(take > 0), rx_w[...].reshape(T, 128))
        xw_w[...] = got[0:64].astype(BF)
        yw[...] = got[64:128].astype(BF)
        dm[...] = got[128:144]
        rxo[outer] = yw[...]
        for d in range(1, N):
            t = (outer + d) % N
            to_outer(yw, rxo.at[outer], yw_s, yw_r, t).start()

    lse_l = top_l[...] + jnp.log(sum_l[...])
    lse_m = sum3(nn(split3(jnp.where(keep_m, lse_l, 0.0)), place_m))
    lse_w = sum3(nn(split3(jnp.where(keep_w, lse_l, 0.0)), place_w))
    row8 = iota((8, 1), 0)
    for h in range(HEADS):
        st_tx[h] = jnp.where(row8 == 0, lse_m[h : h + 1], lse_w[h : h + 1])
    send_to_heads(lambda h: st_tx.at[h], st_rx, st_s, st_r)

    @pl.when(active)
    def _():
        st_rx[inner] = st_tx[head]

    def local_q(h, _):
        acc_q[h] = tn(gl[h], yl[h])
        om, ow = om_ref[h], ow_ref[h]
        r = iota((1, BACK), 1)
        want = jnp.where(r < 64, 4 * r + om, jnp.where((r >= 96) & (r < 100), 64 * (r - 96) + ow, -1))
        where_back[h, 0] = onehot(iota((T, BACK), 0) == want)
        return 0

    lax.fori_loop(0, HEADS, local_q, 0, unroll=3)

    @pl.when(active)
    def _():
        got_inner(rx.at[pl.ds(0, N - 1), pl.ds(0, 64)], mk_r)
        om, ow = om_ref[head], ow_ref[head]
        yk[...] = rx[:, 0:64, :] * half_k
        yv[...] = rx[:, 0:64, :] * half_v

        def mid_a(u):
            b = block_of(3 - u)
            got_inner(rx.at[pl.ds(0, 3 if u == 0 else 4), pl.ds(64, 64)], mq_r.at[b])
            x = rx[pl.ds(4 * b, 4), 64:128, :].reshape(T, 128)
            delta = jnp.concatenate([dm[pl.ds(2 * b, 1), :], dm[pl.ds(2 * b + 1, 1), :]], axis=1)
            top = jnp.full((1, T), NEG, F32)
            for kb in range(4):
                s = nt(yk[4 * kb : 4 * kb + 4].reshape(T, 128), x)
                s_scr[u, kb] = s
                top = jnp.maximum(top, jnp.max(s, axis=0, keepdims=True))
            total = jnp.zeros((1, T), F32)
            dq = jnp.zeros((T, 128), F32)
            for kb in range(4):
                e = jnp.exp(s_scr[u, kb] - top)
                total = total + jnp.sum(e, axis=0, keepdims=True)
                d = nt(yv[4 * kb : 4 * kb + 4].reshape(T, 128), x)
                em[b, kb] = e.astype(BF)
                g = (e * (d - delta)).astype(BF)
                gm[b, kb] = g
                dq = dq + tn(g, rx[4 * kb : 4 * kb + 4, 0:64, :].reshape(T, 128))
            for i in range(4):
                mine = dq[64 * i : 64 * i + 64]
                ret[4 * b + i, 64:96, :] = jnp.where(left, mine[:32], swap(mine[32:])).astype(BF)
            for i in range(2):
                mm[pl.ds(2 * b + i, 1), :] = top[:, 128 * i : 128 * i + 128]
                sm[pl.ds(2 * b + i, 1), :] = total[:, 128 * i : 128 * i + 128]
            for i in range(1 if u == 0 else 0, 4):
                t = 4 * b + (inner + i) % 4
                to_inner(ret.at[t, pl.ds(64, 32)], back.at[head, pl.ds(64, 32)], rq_s, rq_r, t).start()

        for u in range(4):
            mid_a(u)

        got_inner(st_rx.at[pl.ds(0, N - 1)], st_r)
        ones = onehot(iota((8, N), 0) == (iota((8, N), 1) >> 1))
        rows = st_rx[:, 0, :]
        first = rows.astype(BF).astype(F32)
        second = (rows - first).astype(BF).astype(F32)
        third = rows - first - second
        lm[...] = nn(ones, first.astype(BF)) + nn(ones, second.astype(BF)) + nn(ones, third.astype(BF))
        lse_local_w = jnp.sum(st_rx[:, 1, :], axis=0, keepdims=True)
        got_outer(rxo.at[pl.ds(0, N - 1)], yw_r)

        all_y = rxo[...].reshape(N * 64, 128)
        x_w = xw_w[...]
        s = nt(all_y * half_k, x_w)
        top_w = jnp.max(s, axis=0, keepdims=True)
        e = jnp.exp(s - top_w)
        lse_w = top_w + jnp.log(jnp.sum(e, axis=0, keepdims=True))
        d = nt(all_y * half_v, x_w)
        ew = e.astype(BF)
        gw = (e * (d - dm[8:9, 0:64])).astype(BF)
        s = nt(yk[...].reshape(N * 64, 128), x_w)
        top = jnp.max(s, axis=0, keepdims=True)
        m_at_w = top + jnp.log(jnp.sum(jnp.exp(s - top), axis=0, keepdims=True))
        shared = (ow & 3) == om
        spot = jnp.where(shared, ow >> 2, -1)
        spot_row = jnp.full((1, 64), spot, I32)
        total_w = lse3(lse_w, lse_local_w[:, :64], jnp.where(spot_row >= 0, m_at_w, NEG))
        weight_w = jnp.exp(top_w - total_w)
        zeros64 = jnp.zeros((1, 64), F32)
        col_w = jnp.broadcast_to(jnp.concatenate([weight_w, zeros64], axis=1), (128, 128)).T[0:64, 0:1]
        scaled = (x_w.astype(F32) * col_w).astype(BF)
        wp[...] = jnp.where(left, nn(gw, scaled), nn(ew, scaled)).astype(BF).reshape(N, 64, 128)
        rxp[outer] = wp[outer]

        for d in range(1, N):
            t = (outer + d) % N
            to_outer(wp.at[t], rxp.at[outer], wp_s, wp_r, t).start()

        dq_w = (tn(gw, all_y) * col_w).astype(BF)

        lse_w = jnp.concatenate([lse_w, zeros64], axis=1)
        lane8, chunk8 = iota((8, 128), 1), iota((8, 128), 0)
        n128 = iota((128, 128), 1)
        spread = onehot(((n128 & 7) == (iota((128, 128), 0) >> 4)) & (n128 < 64))
        w_at_m = sum3(nt(split3(jnp.where((lane8 >> 3) == chunk8, lse_w, 0.0)), spread))
        wm[...] = jnp.where((lane8 & 15) == spot, w_at_m, NEG)

        lse_m = mm[...] + jnp.log(sm[...])
        weight_m = jnp.exp(mm[...] - lse3(lse_m, lm[...], wm[...]))
        columns = jnp.concatenate([weight_m, jnp.zeros((120, 128), F32)], axis=0).T
        for j in range(8):
            ls_tx[j] = jnp.where(chunk8 == 0, lse_m[j : j + 1], jnp.where(chunk8 == 1, lse_w, mm[j : j + 1, :]))
            col = columns[:, j : j + 1]
            x = rx[2 * j : 2 * j + 2, 64:128, :].reshape(128, 128).astype(F32)
            xw_all[j // 2, 128 * (j % 2) : 128 * (j % 2) + 128, :] = (x * col).astype(BF)
        for d in range(1, N):
            t = (inner + d) % N
            to_inner(ls_tx.at[t // 2], ls_rx.at[head], ls_s, ls_r, t).start()
        ls_rx[head] = ls_tx[inner // 2]

        def mid_b(u, _):
            kb = block_of(u)
            from_g = jnp.zeros((T, 128), F32)
            from_e = jnp.zeros((T, 128), F32)
            for b in range(4):
                x = xw_all[b]
                from_g = from_g + nn(gm[b, kb], x)
                from_e = from_e + nn(em[b, kb], x)
            both = jnp.where(left, from_g, from_e).astype(BF)
            ret[pl.ds(4 * kb, 4), 0:64, :] = both.reshape(4, 64, 128)

            for j in range(4):
                t = 4 * kb + (inner + j) % 4

                @pl.when(t != inner)
                def _():
                    to_inner(ret.at[t, pl.ds(0, 64)], back.at[head, pl.ds(0, 64)], rk_s, rk_r, t).start()

            return 0

        lax.fori_loop(0, 4, mid_b, 0)
        back[head, 0:96, :] = ret[inner]

        got_outer(rxp.at[pl.ds(0, N - 1)], wp_r)
        kv_w = jnp.sum(rxp[...].astype(F32), axis=0).astype(BF)
        r256, n64 = iota((T, 64), 0), iota((T, 64), 1)
        slot = r256 & 15
        at = 4 * (r256 >> 4) + (slot & 3)
        rows_w = nn(onehot((n64 == at) & (slot < 4)), kv_w)
        rows_w = rows_w + nn(onehot((n64 == at) & (slot >= 4) & (slot < 8)), dq_w)
        retw[...] = rows_w.astype(BF).reshape(N, 16, 128)

        for d in range(1, N):
            t = (inner + d) % N
            to_inner(retw.at[t], back.at[head, pl.ds(96, 16)], rw_s, rw_r, t).start()
        back[head, 96:112, :] = retw[inner]

    @pl.when(active)
    def _():
        got_inner(ls_rx.at[pl.ds(0, HEADS - 1)], ls_r)

    @pl.when(jnp.logical_not(active))
    def _():
        got_inner(ls_rx, ls_r)

    pad = jnp.zeros((4, 128), F32)
    lse_m = sum3(nt(split3(jnp.concatenate([ls_rx[:, 0, :], pad], axis=0)), place_m))
    lse_w = sum3(nt(split3(jnp.concatenate([ls_rx[:, 1, :], pad], axis=0)), place_w))
    total = lse3(lse_l, jnp.where(keep_m, lse_m, NEG), jnp.where(keep_w, lse_w, NEG))
    weight = jnp.exp(top_l[...] - total)
    top_m = sum3(nt(split3(jnp.concatenate([ls_rx[:, 2, :], pad], axis=0)), place_m))
    weight_m = jnp.where(keep_m, jnp.exp(jnp.where(keep_m, top_m, NEG) - total), 0.0)
    cols_l[...] = jnp.concatenate([weight, weight_m, jnp.zeros((96, T), F32)], axis=0).T
    for h in range(HEADS):
        col = cols_l[:, h : h + 1]
        x = (xl[h].astype(F32) * col).astype(BF)
        acc_kv[h] = jnp.where(left, nn(gl[h], x), nn(el[h], x))
        acc_q[h] = acc_q[h] * col
        col = cols_l[:, 16 + h : 17 + h]
        r = iota((1, BACK), 1)
        t = iota((T, BACK), 0)
        in_q = (r >= 64) & (r < 96)
        om, ow = om_ref[h], ow_ref[h]
        want_q = jnp.where(
            in_q, 4 * (r - 64) + om, jnp.where((r >= 100) & (r < 104), 64 * (r - 100) + ow, -1)
        )
        want_r = jnp.where(in_q, 4 * (r - 32) + om, -1)
        where_back[h, 1] = jnp.where(t == want_q, jnp.where(in_q, col, 1.0), 0.0).astype(BF)
        where_back[h, 2] = jnp.where(t == want_r, col, 0.0).astype(BF)

    def close(heads):
        got_inner(back.at[pl.ds(0, heads), pl.ds(64, 32)], rq_r)
        got_inner(back.at[pl.ds(0, heads), pl.ds(0, 64)], rk_r)
        got_inner(back.at[pl.ds(0, heads), pl.ds(96, 16)], rw_r)
        sent_inner(msg_w.at[pl.ds(0, heads)], mw_s)
        sent_inner(msg.at[pl.ds(0, heads), pl.ds(0, 64)], mk_s)
        sent_inner(msg.at[pl.ds(0, heads), pl.ds(64, 64)], mq_s)
        sent_inner(st_rx.at[pl.ds(0, heads)], st_s)

    @pl.when(active)
    def _():
        close(HEADS - 1)
        sent_inner(st_rx.at[pl.ds(0, N - 1)], ls_s)
        sent_inner(ret.at[pl.ds(0, N - 1), pl.ds(64, 32)], rq_s)
        sent_inner(ret.at[pl.ds(0, N - 1), pl.ds(0, 64)], rk_s)
        sent_inner(retw.at[pl.ds(0, N - 1)], rw_s)
        sent_outer(rxo.at[pl.ds(0, N - 1)], yw_s)
        sent_outer(wp.at[pl.ds(0, N - 1)], wp_s)

    @pl.when(jnp.logical_not(active))
    def _():
        close(HEADS)


def finish(acc_kv, acc_q, back, where_back, dq_hbm, dk_hbm, dv_hbm, dq_ref, dk_ref, dv_ref, sems):
    left = iota((1, 128), 1) < 64
    copies = []
    for p in range(HEADS // 2):
        cols = pl.ds(p * 128, 128)
        kvs, qs, rest = [], [], []
        for a in range(2):
            h = 2 * p + a
            rows = back[h]
            kvs.append(acc_kv[h] + nn(where_back[h, 0], rows))
            qs.append(acc_q[h] + nn(where_back[h, 1], rows))
            rest.append(nn(where_back[h, 2], rows))
        dq = jnp.where(left, qs[0] + swap(rest[0]), swap(qs[1]) + rest[1])
        dq_ref[:, cols] = (SCALE * dq).astype(BF)
        dk_ref[:, cols] = (SCALE * jnp.where(left, kvs[0], swap(kvs[1]))).astype(BF)
        dv_ref[:, cols] = jnp.where(left, swap(kvs[0]), kvs[1]).astype(BF)
        if p % 2 == 1:
            wide = pl.ds((p - 1) * 128, 256)
            for i, (src, dst) in enumerate([(dq_ref, dq_hbm), (dk_ref, dk_hbm), (dv_ref, dv_hbm)]):
                copies.append(pltpu.make_async_copy(src.at[:, wide], dst.at[:, wide], sems.at[i, p // 2]))
                copies[-1].start()
    for copy in copies:
        copy.wait()


def per_device(queries, keys, values, saved_out, out_grad, offset_mid, offset_wide):
    vmem = pl.BlockSpec(memory_space=pltpu.VMEM)
    hbm = pl.BlockSpec(memory_space=pltpu.HBM)
    v = pltpu.VMEM
    dma = pltpu.SemaphoreType.DMA
    rows = jax.ShapeDtypeStruct((T, HEADS * 64), BF)
    parts = pl.pallas_call(
        kernel,
        out_shape=(
            jax.ShapeDtypeStruct((HEADS, T, 128), F32),
            jax.ShapeDtypeStruct((HEADS, T, 128), F32),
            jax.ShapeDtypeStruct((HEADS, BACK, 128), BF),
            jax.ShapeDtypeStruct((HEADS, 3, T, BACK), BF),
        ),
        in_specs=[hbm] * 7,
        out_specs=(vmem,) * 4,
        scratch_shapes=[
            pltpu.SMEM((HEADS,), I32),
            pltpu.SMEM((HEADS,), I32),
            v((T, HEADS * 64), BF),
            v((T, HEADS * 64), BF),
            v((T, HEADS * 64), BF),
            v((T, HEADS * 64), BF),
            v((T, HEADS * 64), BF),
            v((HEADS, T, 128), BF),
            v((HEADS, T, 128), BF),
            v((HEADS, 16, 128), BF),
            v((HEADS, 128, 128), BF),
            v((N, 16, 128), BF),
            v((N, 128, 128), BF),
            v((HEADS, T, T), BF),
            v((HEADS, T, T), BF),
            v((16, T), F32),
            v((16, T), F32),
            v((16, T), F32),
            v((T, 128), F32),
            v((HEADS, 8, 128), F32),
            v((N, 8, 128), F32),
            v((8, 8, 128), F32),
            v((HEADS, 8, 128), F32),
            v((N, 64, 128), BF),
            v((N, 64, 128), BF),
            v((4, 4, T, T), F32),
            v((4, 4, T, T), BF),
            v((4, 4, T, T), BF),
            v((8, 128), F32),
            v((8, 128), F32),
            v((16, 128), F32),
            v((8, 128), F32),
            v((8, 128), F32),
            v((4, T, 128), BF),
            v((64, 128), BF),
            v((64, 128), BF),
            v((N, 64, 128), BF),
            v((N, 64, 128), BF),
            v((N, 64, 128), BF),
            v((N, 96, 128), BF),
            v((N, 16, 128), BF),
            dma((7,)),
            dma, dma,
            dma, dma,
            dma, dma((4,)),
            dma, dma,
            dma, dma,
            dma, dma,
            dma, dma,
            dma, dma,
            dma, dma,
            dma, dma,
        ],
        compiler_params=pltpu.CompilerParams(
            collective_id=0, has_side_effects=True, vmem_limit_bytes=44 * 1024 * 1024
        ),
    )(
        *[
            pltpu.with_memory_space_constraint(x, pltpu.HBM)
            for x in (offset_mid, offset_wide, queries, keys, values, saved_out, out_grad)
        ]
    )
    return pl.pallas_call(
        finish,
        out_shape=(rows, rows, rows),
        in_specs=[vmem] * 4,
        out_specs=(hbm,) * 3,
        scratch_shapes=[v((T, HEADS * 64), BF)] * 3 + [dma((3, 3))],
        compiler_params=pltpu.CompilerParams(vmem_limit_bytes=40 * 1024 * 1024),
    )(*parts)


def solution(mesh):
    rows = P(("outer", "inner"), None)
    return jax.shard_map(
        per_device,
        mesh=mesh,
        in_specs=(rows, rows, rows, rows, rows, P(), P()),
        out_specs=(rows, rows, rows),
        check_vma=False,
    )
```

```python
import jax
import jax.numpy as jnp
from jax import lax
from jax.experimental import pallas as pl
from jax.experimental.pallas import tpu as pltpu
from jax.sharding import PartitionSpec as P

BF = jnp.bfloat16
F32 = jnp.float32
I32 = jnp.int32

N = 16
FAR = (8, 9, 10, 7, 6, 11, 12, 5, 4, 13, 14, 3, 2, 15, 1)
HEADS = 12
T = 256
MID = 64
SCALE = 0.125
NEG = -1e30
BACK = 96


def iota(shape, dim):
    return lax.broadcasted_iota(I32, shape, dim)


def nn(a, b):
    return lax.dot_general(a, b, (((1,), (0,)), ((), ())), preferred_element_type=F32)


def nt(a, b):
    return lax.dot_general(a, b, (((1,), (1,)), ((), ())), preferred_element_type=F32)


def tn(a, b):
    return lax.dot_general(a, b, (((0,), (0,)), ((), ())), preferred_element_type=F32)


def onehot(mask):
    return jnp.where(mask, 1.0, 0.0).astype(BF)


def split3(x):
    a = x.astype(BF).astype(F32)
    r = x - a
    b = r.astype(BF).astype(F32)
    return jnp.concatenate([a, b, r - b], axis=0).astype(BF)


def sum3(x):
    r = x.shape[0] // 3
    return x[:r] + x[r : 2 * r] + x[2 * r :]


def lse3(a, b, c):
    top = jnp.maximum(a, jnp.maximum(b, c))
    return top + jnp.log(jnp.exp(a - top) + jnp.exp(b - top) + jnp.exp(c - top))


def swap(x):
    return pltpu.roll(x, 64, 1)


def kernel(
    om_hbm, ow_hbm, q_hbm, k_hbm, v_hbm, o_hbm, g_hbm,
    fin_q, fin_k, fin_v, back_w, places_w,
    om_ref, ow_ref, q_ref, k_ref, v_ref, o_ref, g_ref,
    acc_kv, acc_q, back, where_kv, where_q, xl, yl, msg_w, msg, rx_w, rx, el, gl, dl, top_l, sum_l, cols_l, st_tx, st_rx, ls_tx, ls_rx,
    yk, yv, s_scr, em, gm, mm, sm, dm, lm, wm, xw_all, xw_w, yw, rxo, wp, rxp, lw, dqw, ret, retw,
    in_s, mw_s, mw_r, mk_s, mk_r, mq_s, mq_r, st_s, st_r, ls_s, ls_r, yw_s, yw_r, wp_s, wp_r,
    rk_s, rk_r, rq_s, rq_r, rw_s, rw_r,
):
    inner = lax.axis_index("inner")
    outer = lax.axis_index("outer")
    quad = inner // 4
    active = inner % 4 < 3
    head = jnp.minimum(quad * 3 + inner % 4, HEADS - 1)

    def to_inner(src, dst, send, recv, target):
        return pltpu.make_async_remote_copy(
            src_ref=src, dst_ref=dst, send_sem=send, recv_sem=recv,
            device_id={"inner": target}, device_id_type=pl.DeviceIdType.MESH,
        )

    def to_outer(src, dst, send, recv, target):
        return pltpu.make_async_remote_copy(
            src_ref=src, dst_ref=dst, send_sem=send, recv_sem=recv,
            device_id={"outer": target}, device_id_type=pl.DeviceIdType.MESH,
        )

    loads = [
        pltpu.make_async_copy(src, dst, in_s.at[i])
        for i, (src, dst) in enumerate(
            [
                (om_hbm, om_ref), (ow_hbm, ow_ref), (q_hbm, q_ref), (g_hbm, g_ref),
                (k_hbm, k_ref), (v_hbm, v_ref), (o_hbm, o_ref),
            ]
        )
    ]
    barrier = pltpu.get_barrier_semaphore()

    for load in loads:
        load.start()

    def greet(d, _):
        pl.semaphore_signal(
            barrier, inc=1, device_id={"inner": (inner + d) % N}, device_id_type=pl.DeviceIdType.MESH
        )
        pl.semaphore_signal(
            barrier, inc=1, device_id={"outer": (outer + d) % N}, device_id_type=pl.DeviceIdType.MESH
        )
        return 0

    lax.fori_loop(1, N, greet, 0)
    for load in loads:
        load.wait()

    left = iota((1, 128), 1) < 64
    half_k = jnp.where(left, SCALE, 0.0).astype(BF)
    half_v = jnp.where(left, 0.0, 1.0).astype(BF)

    def block_of(u):
        return (quad // 2 + 1 - u // 2) % 2 * 2 + (quad + 1 - u % 2) % 2

    def peers():
        return [4 * block_of(i // 4) + (inner + i) % 4 for i in range(N) if i != 12]

    t_row = iota((T, 128), 0)
    t_lane = iota((T, 128), 1)
    place_m = onehot(t_lane == (t_row >> 2) + 64 * (inner % 2))
    place_w = onehot(t_lane == (t_row >> 6) + 4 * inner)
    tok = iota((1, T), 1)
    head_row = iota((16, 1), 0)
    om_col, ow_col = jnp.zeros((16, 1), I32), jnp.zeros((16, 1), I32)
    for h in range(HEADS):
        om_col = jnp.where(head_row == h, om_ref[h], om_col)
        ow_col = jnp.where(head_row == h, ow_ref[h], ow_col)
    keep_m = (tok & 3) == om_col
    keep_w = (tok & 63) == ow_col

    prod = g_ref[...].astype(F32) * o_ref[...].astype(F32)
    hi = prod.astype(BF)
    lo = (prod - hi.astype(F32)).astype(BF)
    of_head = onehot(iota((16, HEADS * 64), 0) == (iota((16, HEADS * 64), 1) >> 6))
    delta = nt(of_head, hi) + nt(of_head, lo)
    dl[...] = delta
    delta_m = nn(split3(jnp.where(keep_m, delta, 0.0)), place_m)
    delta_w = nn(split3(jnp.where(keep_w, delta, 0.0)), place_w)

    row16 = iota((16, 1), 0)
    for p in range(HEADS // 2):
        cols = pl.ds(p * 128, 128)
        qp, kp, vp, gp = q_ref[:, cols], k_ref[:, cols], v_ref[:, cols], g_ref[:, cols]
        for a in range(2):
            h = 2 * p + a
            b, c = 64 * a, 64 * a + 64
            x = jnp.concatenate([qp[:, b:c], gp[:, b:c]], axis=1)
            y = jnp.concatenate([kp[:, b:c], vp[:, b:c]], axis=1)
            xl[h] = x
            yl[h] = y
            om, ow = om_ref[h], ow_ref[h]
            row = iota((96, 1), 0)
            r = row - 64
            w = r & 15
            wide = jnp.where((r < 16) & (w < 4), 64 * w + ow, -1)
            wide = jnp.where((r >= 16) & (w >= 4) & (w < 8), 64 * (w - 4) + ow, wide)
            want = jnp.where(row < 64, 4 * row + om, wide)
            pick = onehot(iota((96, T), 1) == want)
            got = nn(pick, jnp.concatenate([x, y], axis=1))
            msg[h, 0:64, :] = got[0:64, 128:256].astype(BF)
            msg[h, 64:128, :] = got[0:64, 0:128].astype(BF)
            tile = got[64:80, 0:128] + got[80:96, 128:256]
            for i in range(3):
                tile = jnp.where(row16 == 8 + i, delta_m[16 * i + h : 16 * i + h + 1], tile)
                tile = jnp.where(row16 == 11 + i, delta_w[16 * i + h : 16 * i + h + 1], tile)
            msg_w[h] = tile.astype(BF)
    pl.semaphore_wait(barrier, 2 * (N - 1))

    def block_of(u):
        return (quad // 2 + 1 - u // 2) % 2 * 2 + (quad + 1 - u % 2) % 2

    def send_to_heads(src_of, dst, send, recv, rows=None):
        place = dst.at[inner] if rows is None else dst.at[inner, rows]
        for i in range(HEADS):
            block = block_of(i // 3)
            j = (i + inner) % 3
            h, target = 3 * block + j, 4 * block + j
            if i < 9:
                to_inner(src_of(h), place, send, recv, target).start()
            else:

                @pl.when(target != inner)
                def _():
                    to_inner(src_of(h), place, send, recv, target).start()

    def got_inner(dst, recv):
        to_inner(dst, dst, recv, recv, (inner + 1) % N).wait_recv()

    def got_outer(dst, recv):
        to_outer(dst, dst, recv, recv, (outer + 1) % N).wait_recv()

    def sent_inner(src, send):
        to_inner(src, src, send, send, (inner + 1) % N).wait_send()

    def sent_outer(src, send):
        to_outer(src, src, send, send, (outer + 1) % N).wait_send()

    send_to_heads(lambda h: msg_w.at[h], rx_w, mw_s, mw_r)
    send_to_heads(lambda h: msg.at[h, pl.ds(0, 64)], rx, mk_s, mk_r, pl.ds(0, 64))
    send_to_heads(lambda h: msg.at[h, pl.ds(64, 64)], rx, mq_s, mq_r.at[quad], pl.ds(64, 64))

    @pl.when(active)
    def _():
        rx_w[inner] = msg_w[head]
        rx[inner] = msg[head]

    top_l[...] = jnp.zeros((16, T), F32)
    sum_l[...] = jnp.ones((16, T), F32)

    def local_a(h, _):
        x, y = xl[h], yl[h]
        s = nt(y * half_k, x)
        top = jnp.max(s, axis=0, keepdims=True)
        e = jnp.exp(s - top)
        top_l[pl.ds(h, 1), :] = top
        sum_l[pl.ds(h, 1), :] = jnp.sum(e, axis=0, keepdims=True)
        d = nt(y * half_v, x)
        el[h] = e.astype(BF)
        gl[h] = (e * (d - dl[pl.ds(h, 1), :])).astype(BF)
        return 0

    lax.fori_loop(0, HEADS, local_a, 0, unroll=3)
    @pl.when(active)
    def _():
        got_inner(rx_w.at[pl.ds(0, N - 1)], mw_r)
        r, c = iota((144, T), 0), iota((144, T), 1)
        slot, owner = c & 15, c >> 4
        at = 16 * ((r & 63) >> 2) + (r & 3)
        j = r - 128
        take = jnp.where(r < 64, jnp.where(c == at, 1, 0), jnp.where(c == at + 4, 1, 0))
        in_m = jnp.where((slot >= 8) & (slot < 11) & ((owner >> 1) == j), 1, 0)
        in_w = jnp.where((slot >= 11) & (slot < 14) & (j == 8), 1, 0)
        take = jnp.where(r < 128, take, in_m + in_w)
        got = nn(onehot(take > 0), rx_w[...].reshape(T, 128))
        xw_w[...] = got[0:64].astype(BF)
        yw[...] = got[64:128].astype(BF)
        dm[...] = got[128:144]
        rxo[outer] = yw[...]
        for d in FAR:
            t = (outer + d) % N
            to_outer(yw, rxo.at[outer], yw_s, yw_r, t).start()

    lse_l = top_l[...] + jnp.log(sum_l[...])
    lse_m = sum3(nn(split3(jnp.where(keep_m, lse_l, 0.0)), place_m))
    lse_w = sum3(nn(split3(jnp.where(keep_w, lse_l, 0.0)), place_w))
    row8 = iota((8, 1), 0)
    for h in range(HEADS):
        st_tx[h] = jnp.where(row8 == 0, lse_m[h : h + 1], lse_w[h : h + 1])
    send_to_heads(lambda h: st_tx.at[h], st_rx, st_s, st_r)

    @pl.when(active)
    def _():
        st_rx[inner] = st_tx[head]

    def local_q(h, _):
        acc_q[h] = tn(gl[h], yl[h])
        where_kv[h] = onehot(iota((T, 64), 0) == 4 * iota((1, 64), 1) + om_ref[h])
        return 0

    lax.fori_loop(0, HEADS, local_q, 0, unroll=3)

    @pl.when(active)
    def _():
        got_inner(rx.at[pl.ds(0, N - 1), pl.ds(0, 64)], mk_r)
        om, ow = om_ref[head], ow_ref[head]
        yk[...] = rx[:, 0:64, :] * half_k
        yv[...] = rx[:, 0:64, :] * half_v

        x_w = xw_w[...]
        s = nt(yk[...].reshape(N * 64, 128), x_w)
        top = jnp.max(s, axis=0, keepdims=True)
        m_at_w = top + jnp.log(jnp.sum(jnp.exp(s - top), axis=0, keepdims=True))

        def mid_a(u):
            b = block_of(3 - u)
            got_inner(rx.at[pl.ds(0, 3 if u == 0 else 4), pl.ds(64, 64)], mq_r.at[b])
            x = rx[pl.ds(4 * b, 4), 64:128, :].reshape(T, 128)
            delta = jnp.concatenate([dm[pl.ds(2 * b, 1), :], dm[pl.ds(2 * b + 1, 1), :]], axis=1)
            top = jnp.full((1, T), NEG, F32)
            for kb in range(4):
                s = nt(yk[4 * kb : 4 * kb + 4].reshape(T, 128), x)
                s_scr[u, kb] = s
                top = jnp.maximum(top, jnp.max(s, axis=0, keepdims=True))
            total = jnp.zeros((1, T), F32)
            dq = jnp.zeros((T, 128), F32)
            for kb in range(4):
                e = jnp.exp(s_scr[u, kb] - top)
                total = total + jnp.sum(e, axis=0, keepdims=True)
                d = nt(yv[4 * kb : 4 * kb + 4].reshape(T, 128), x)
                em[b, kb] = e.astype(BF)
                g = (e * (d - delta)).astype(BF)
                gm[b, kb] = g
                dq = dq + tn(g, rx[4 * kb : 4 * kb + 4, 0:64, :].reshape(T, 128))
            for i in range(4):
                mine = dq[64 * i : 64 * i + 64]
                ret[4 * b + i, 64:96, :] = jnp.where(left, mine[:32], swap(mine[32:])).astype(BF)
            for i in range(2):
                mm[pl.ds(2 * b + i, 1), :] = top[:, 128 * i : 128 * i + 128]
                sm[pl.ds(2 * b + i, 1), :] = total[:, 128 * i : 128 * i + 128]
            for i in range(1 if u == 0 else 0, 4):
                t = 4 * b + (inner + i) % 4
                to_inner(ret.at[t, pl.ds(64, 32)], back.at[head, pl.ds(64, 32)], rq_s, rq_r, t).start()

        lane8, chunk8 = iota((8, 128), 1), iota((8, 128), 0)

        def wide():
            got_inner(st_rx.at[pl.ds(0, N - 1)], st_r)
            ones = onehot(iota((8, N), 0) == (iota((8, N), 1) >> 1))
            rows = st_rx[:, 0, :]
            first = rows.astype(BF).astype(F32)
            second = (rows - first).astype(BF).astype(F32)
            third = rows - first - second
            lm[...] = nn(ones, first.astype(BF)) + nn(ones, second.astype(BF)) + nn(ones, third.astype(BF))
            lse_local_w = jnp.sum(st_rx[:, 1, :], axis=0, keepdims=True)
            got_outer(rxo.at[pl.ds(0, N - 1)], yw_r)

            all_y = rxo[...].reshape(N * 64, 128)
            s = nt(all_y * half_k, x_w)
            top_w = jnp.max(s, axis=0, keepdims=True)
            e = jnp.exp(s - top_w)
            lse_w = top_w + jnp.log(jnp.sum(e, axis=0, keepdims=True))
            d = nt(all_y * half_v, x_w)
            ew = e.astype(BF)
            gw = (e * (d - dm[8:9, 0:64])).astype(BF)
            shared = (ow & 3) == om
            spot = jnp.where(shared, ow >> 2, -1)
            spot_row = jnp.full((1, 64), spot, I32)
            total_w = lse3(lse_w, lse_local_w[:, :64], jnp.where(spot_row >= 0, m_at_w, NEG))
            weight_w = jnp.exp(top_w - total_w)
            zeros64 = jnp.zeros((1, 64), F32)
            col_w = jnp.broadcast_to(jnp.concatenate([weight_w, zeros64], axis=1), (128, 128)).T[0:64, 0:1]
            scaled = (x_w.astype(F32) * col_w).astype(BF)
            wp[...] = jnp.where(left, nn(gw, scaled), nn(ew, scaled)).astype(BF).reshape(N, 64, 128)
            rxp[outer] = wp[outer]

            for d in FAR:
                t = (outer + d) % N
                to_outer(wp.at[t], rxp.at[outer], wp_s, wp_r, t).start()

            dqw[...] = (tn(gw, all_y) * col_w).astype(BF)

            lse_w = jnp.concatenate([lse_w, zeros64], axis=1)
            lw[...] = jnp.broadcast_to(lse_w, (8, 128))
            n128 = iota((128, 128), 1)
            spread = onehot(((n128 & 7) == (iota((128, 128), 0) >> 4)) & (n128 < 64))
            w_at_m = sum3(nt(split3(jnp.where((lane8 >> 3) == chunk8, lse_w, 0.0)), spread))
            wm[...] = jnp.where((lane8 & 15) == spot, w_at_m, NEG)

        late = outer >= 8
        for u in range(4):
            if u == 3:
                pl.when(late)(wide)
            mid_a(u)
        pl.when(jnp.logical_not(late))(wide)

        lse_m = mm[...] + jnp.log(sm[...])
        weight_m = jnp.exp(mm[...] - lse3(lse_m, lm[...], wm[...]))
        columns = jnp.concatenate([weight_m, jnp.zeros((120, 128), F32)], axis=0).T
        for j in range(8):
            ls_tx[j] = jnp.where(chunk8 == 0, lse_m[j : j + 1], jnp.where(chunk8 == 1, lw[...], mm[j : j + 1, :]))
            col = columns[:, j : j + 1]
            x = rx[2 * j : 2 * j + 2, 64:128, :].reshape(128, 128).astype(F32)
            xw_all[j // 2, 128 * (j % 2) : 128 * (j % 2) + 128, :] = (x * col).astype(BF)
        for t in peers():
            to_inner(ls_tx.at[t // 2], ls_rx.at[head], ls_s, ls_r, t).start()
        ls_rx[head] = ls_tx[inner // 2]

        def mid_b(u, _):
            kb = block_of(u)
            from_g = jnp.zeros((T, 128), F32)
            from_e = jnp.zeros((T, 128), F32)
            for b in range(4):
                x = xw_all[b]
                from_g = from_g + nn(gm[b, kb], x)
                from_e = from_e + nn(em[b, kb], x)
            both = jnp.where(left, from_g, from_e).astype(BF)
            ret[pl.ds(4 * kb, 4), 0:64, :] = both.reshape(4, 64, 128)

            for j in range(4):
                t = 4 * kb + (inner + j) % 4

                @pl.when(t != inner)
                def _():
                    to_inner(ret.at[t, pl.ds(0, 64)], back.at[head, pl.ds(0, 64)], rk_s, rk_r, t).start()

            return 0

        lax.fori_loop(0, 4, mid_b, 0)
        back[head, 0:96, :] = ret[inner]

        got_outer(rxp.at[pl.ds(0, N - 1)], wp_r)
        kv_w = jnp.sum(rxp[...].astype(F32), axis=0).astype(BF)
        r256, n64 = iota((T, 64), 0), iota((T, 64), 1)
        slot = r256 & 15
        at = 4 * (r256 >> 4) + (slot & 3)
        rows_w = nn(onehot((n64 == at) & (slot < 4)), kv_w)
        rows_w = rows_w + nn(onehot((n64 == at) & (slot >= 4) & (slot < 8)), dqw[...])
        retw[...] = rows_w.astype(BF).reshape(N, 16, 128)

        for t in peers():
            to_inner(retw.at[t], back_w.at[head], rw_s, rw_r, t).start()
        back_w[head] = retw[inner]

    @pl.when(active)
    def _():
        got_inner(ls_rx.at[pl.ds(0, HEADS - 1)], ls_r)

    @pl.when(jnp.logical_not(active))
    def _():
        got_inner(ls_rx, ls_r)

    pad = jnp.zeros((4, 128), F32)
    lse_m = sum3(nt(split3(jnp.concatenate([ls_rx[:, 0, :], pad], axis=0)), place_m))
    lse_w = sum3(nt(split3(jnp.concatenate([ls_rx[:, 1, :], pad], axis=0)), place_w))
    total = lse3(lse_l, jnp.where(keep_m, lse_m, NEG), jnp.where(keep_w, lse_w, NEG))
    weight = jnp.exp(top_l[...] - total)
    top_m = sum3(nt(split3(jnp.concatenate([ls_rx[:, 2, :], pad], axis=0)), place_m))
    weight_m = jnp.where(keep_m, jnp.exp(jnp.where(keep_m, top_m, NEG) - total), 0.0)
    cols_l[...] = jnp.concatenate([weight, weight_m, jnp.zeros((96, T), F32)], axis=0).T
    for h in range(HEADS):
        col = cols_l[:, h : h + 1]
        x = (xl[h].astype(F32) * col).astype(BF)
        acc_kv[h] = jnp.where(left, nn(gl[h], x), nn(el[h], x))
        acc_q[h] = acc_q[h] * col
        col = cols_l[:, 16 + h : 17 + h]
        r = iota((1, 32), 1)
        t = iota((T, 32), 0)
        where_q[h, 0] = jnp.where(t == 4 * r + om_ref[h], col, 0.0).astype(BF)
        where_q[h, 1] = jnp.where(t == 4 * (r + 32) + om_ref[h], col, 0.0).astype(BF)

    c = iota((1, 192), 1)
    ow_c = jnp.zeros((1, 192), I32)
    for h in range(HEADS):
        ow_c = jnp.where((c >> 4) == h, ow_ref[h], ow_c)
    r = c & 15
    t = iota((T, 192), 0)
    places_w[0:T, :] = onehot(t == jnp.where(r < 4, 64 * r + ow_c, -1))
    places_w[T:, :] = onehot(t == jnp.where((r >= 4) & (r < 8), 64 * (r - 4) + ow_c, -1))

    @pl.when(active)
    def _():
        got_inner(back.at[pl.ds(0, HEADS - 1), pl.ds(64, 32)], rq_r)
        got_inner(back.at[pl.ds(0, HEADS - 1), pl.ds(0, 64)], rk_r)

    @pl.when(jnp.logical_not(active))
    def _():
        got_inner(back.at[pl.ds(0, HEADS), pl.ds(64, 32)], rq_r)
        got_inner(back.at[pl.ds(0, HEADS), pl.ds(0, 64)], rk_r)

    for p in range(HEADS // 2):
        cols = pl.ds(p * 128, 128)
        kvs, qs, rest = [], [], []
        for h in (2 * p, 2 * p + 1):
            kvs.append(acc_kv[h] + nn(where_kv[h], back[h, 0:64, :]))
            qs.append(acc_q[h] + nn(where_q[h, 0], back[h, 64:96, :]))
            rest.append(nn(where_q[h, 1], back[h, 64:96, :]))
        fin_q[:, cols] = jnp.where(left, qs[0] + swap(rest[0]), swap(qs[1]) + rest[1])
        fin_k[:, cols] = jnp.where(left, kvs[0], swap(kvs[1]))
        fin_v[:, cols] = jnp.where(left, swap(kvs[0]), kvs[1])

    def close(heads):
        got_inner(back_w.at[pl.ds(0, heads)], rw_r)
        sent_inner(msg_w.at[pl.ds(0, heads)], mw_s)
        sent_inner(msg.at[pl.ds(0, heads), pl.ds(0, 64)], mk_s)
        sent_inner(msg.at[pl.ds(0, heads), pl.ds(64, 64)], mq_s)
        sent_inner(st_rx.at[pl.ds(0, heads)], st_s)

    @pl.when(active)
    def _():
        close(HEADS - 1)
        sent_inner(st_rx.at[pl.ds(0, N - 1)], ls_s)
        sent_inner(ret.at[pl.ds(0, N - 1), pl.ds(64, 32)], rq_s)
        sent_inner(ret.at[pl.ds(0, N - 1), pl.ds(0, 64)], rk_s)
        sent_inner(retw.at[pl.ds(0, N - 1)], rw_s)
        sent_outer(rxo.at[pl.ds(0, N - 1)], yw_s)
        sent_outer(wp.at[pl.ds(0, N - 1)], wp_s)

    @pl.when(jnp.logical_not(active))
    def _():
        close(HEADS)


def finish(fin_q, fin_k, fin_v, back_w, places_w, dq_hbm, dk_hbm, dv_hbm, rk, rv, dq_ref, dk_ref, dv_ref, sems):
    left = iota((1, 128), 1) < 64
    rk[...] = jnp.zeros_like(rk)
    rv[...] = jnp.zeros_like(rv)
    for p in range(HEADS // 2):
        cols = pl.ds(p * 128, 128)
        a, b = back_w[2 * p].astype(F32), back_w[2 * p + 1].astype(F32)
        rk[32 * p : 32 * p + 16, cols] = jnp.where(left, a, 0.0).astype(BF)
        rk[32 * p + 16 : 32 * p + 32, cols] = jnp.where(left, 0.0, swap(b)).astype(BF)
        rv[32 * p : 32 * p + 16, cols] = jnp.where(left, swap(a), 0.0).astype(BF)
        rv[32 * p + 16 : 32 * p + 32, cols] = jnp.where(left, 0.0, b).astype(BF)
    copies = []
    for g in range(3):
        cols = pl.ds(256 * g, 256)
        kq = nn(places_w[...], rk[:, cols])
        dk_ref[:, cols] = (SCALE * (fin_k[:, cols] + kq[:T])).astype(BF)
        dq_ref[:, cols] = (SCALE * (fin_q[:, cols] + kq[T:])).astype(BF)
        dv_ref[:, cols] = (fin_v[:, cols] + nn(places_w[0:T, :], rv[:, cols])).astype(BF)
        for i, (src, dst) in enumerate([(dq_ref, dq_hbm), (dk_ref, dk_hbm), (dv_ref, dv_hbm)]):
            copies.append(pltpu.make_async_copy(src.at[:, cols], dst.at[:, cols], sems.at[i, g]))
            copies[-1].start()
    for copy in copies:
        copy.wait()


def per_device(queries, keys, values, saved_out, out_grad, offset_mid, offset_wide):
    vmem = pl.BlockSpec(memory_space=pltpu.VMEM)
    hbm = pl.BlockSpec(memory_space=pltpu.HBM)
    v = pltpu.VMEM
    dma = pltpu.SemaphoreType.DMA
    rows = jax.ShapeDtypeStruct((T, HEADS * 64), BF)
    parts = pl.pallas_call(
        kernel,
        out_shape=(
            jax.ShapeDtypeStruct((T, HEADS * 64), F32),
            jax.ShapeDtypeStruct((T, HEADS * 64), F32),
            jax.ShapeDtypeStruct((T, HEADS * 64), F32),
            jax.ShapeDtypeStruct((HEADS, 16, 128), BF),
            jax.ShapeDtypeStruct((2 * T, HEADS * 16), BF),
        ),
        in_specs=[hbm] * 7,
        out_specs=(vmem,) * 5,
        scratch_shapes=[
            pltpu.SMEM((HEADS,), I32),
            pltpu.SMEM((HEADS,), I32),
            v((T, HEADS * 64), BF),
            v((T, HEADS * 64), BF),
            v((T, HEADS * 64), BF),
            v((T, HEADS * 64), BF),
            v((T, HEADS * 64), BF),
            v((HEADS, T, 128), F32),
            v((HEADS, T, 128), F32),
            v((HEADS, BACK, 128), BF),
            v((HEADS, T, 64), BF),
            v((HEADS, 2, T, 32), BF),
            v((HEADS, T, 128), BF),
            v((HEADS, T, 128), BF),
            v((HEADS, 16, 128), BF),
            v((HEADS, 128, 128), BF),
            v((N, 16, 128), BF),
            v((N, 128, 128), BF),
            v((HEADS, T, T), BF),
            v((HEADS, T, T), BF),
            v((16, T), F32),
            v((16, T), F32),
            v((16, T), F32),
            v((T, 128), F32),
            v((HEADS, 8, 128), F32),
            v((N, 8, 128), F32),
            v((8, 8, 128), F32),
            v((HEADS, 8, 128), F32),
            v((N, 64, 128), BF),
            v((N, 64, 128), BF),
            v((4, 4, T, T), F32),
            v((4, 4, T, T), BF),
            v((4, 4, T, T), BF),
            v((8, 128), F32),
            v((8, 128), F32),
            v((16, 128), F32),
            v((8, 128), F32),
            v((8, 128), F32),
            v((4, T, 128), BF),
            v((64, 128), BF),
            v((64, 128), BF),
            v((N, 64, 128), BF),
            v((N, 64, 128), BF),
            v((N, 64, 128), BF),
            v((8, 128), F32),
            v((64, 128), BF),
            v((N, 96, 128), BF),
            v((N, 16, 128), BF),
            dma((7,)),
            dma, dma,
            dma, dma,
            dma, dma((4,)),
            dma, dma,
            dma, dma,
            dma, dma,
            dma, dma,
            dma, dma,
            dma, dma,
            dma, dma,
        ],
        compiler_params=pltpu.CompilerParams(
            collective_id=0, has_side_effects=True, vmem_limit_bytes=48 * 1024 * 1024
        ),
    )(
        *[
            pltpu.with_memory_space_constraint(x, pltpu.HBM)
            for x in (offset_mid, offset_wide, queries, keys, values, saved_out, out_grad)
        ]
    )
    return pl.pallas_call(
        finish,
        out_shape=(rows, rows, rows),
        in_specs=[vmem] * 5,
        out_specs=(hbm,) * 3,
        scratch_shapes=[v((HEADS * 16, HEADS * 64), BF)] * 2 + [v((T, HEADS * 64), BF)] * 3 + [dma((3, 3))],
        compiler_params=pltpu.CompilerParams(vmem_limit_bytes=40 * 1024 * 1024),
    )(*parts)


def solution(mesh):
    rows = P(("outer", "inner"), None)
    return jax.shard_map(
        per_device,
        mesh=mesh,
        in_specs=(rows, rows, rows, rows, rows, P(), P()),
        out_specs=(rows, rows, rows),
        check_vma=False,
    )
```

```python
import jax
import jax.numpy as jnp
from jax import lax
from jax.experimental import pallas as pl
from jax.experimental.pallas import tpu as pltpu
from jax.sharding import PartitionSpec as P

BF = jnp.bfloat16
F32 = jnp.float32
I32 = jnp.int32

N = 16
FAR = (8, 9, 10, 7, 6, 11, 12, 5, 4, 13, 14, 3, 2, 15, 1)
HEADS = 12
T = 256
MID = 64
SCALE = 0.125
NEG = -1e30
BACK = 96


def iota(shape, dim):
    return lax.broadcasted_iota(I32, shape, dim)


def nn(a, b):
    return lax.dot_general(a, b, (((1,), (0,)), ((), ())), preferred_element_type=F32)


def nt(a, b):
    return lax.dot_general(a, b, (((1,), (1,)), ((), ())), preferred_element_type=F32)


def tn(a, b):
    return lax.dot_general(a, b, (((0,), (0,)), ((), ())), preferred_element_type=F32)


def onehot(mask):
    return jnp.where(mask, 1.0, 0.0).astype(BF)


def split3(x):
    a = x.astype(BF).astype(F32)
    r = x - a
    b = r.astype(BF).astype(F32)
    return jnp.concatenate([a, b, r - b], axis=0).astype(BF)


def sum3(x):
    r = x.shape[0] // 3
    return x[:r] + x[r : 2 * r] + x[2 * r :]


def lse3(a, b, c):
    top = jnp.maximum(a, jnp.maximum(b, c))
    return top + jnp.log(jnp.exp(a - top) + jnp.exp(b - top) + jnp.exp(c - top))


def swap(x):
    return pltpu.roll(x, 64, 1)


def kernel(
    om_hbm, ow_hbm, q_hbm, k_hbm, v_hbm, o_hbm, g_hbm,
    fin_q, fin_k, fin_v, back_w, places_w,
    om_ref, ow_ref, q_ref, k_ref, v_ref, o_ref, g_ref,
    acc_kv, acc_q, back, where_kv, where_q, xl, yl, msg_w, msg, rx_w, rx, el, gl, dl, top_l, sum_l, cols_l, st_tx, st_rx, ls_tx, ls_rx,
    yk, yv, s_scr, em, gm, mm, sm, dm, lm, wm, xw_all, xw_w, yw, rxo, wp, rxp, lw, dqw, ret, retw,
    in_s, mw_s, mw_r, mk_s, mk_r, mq_s, mq_r, st_s, st_r, ls_s, ls_r, yw_s, yw_r, wp_s, wp_r,
    rk_s, rk_r, rq_s, rq_r, rw_s, rw_r,
):
    inner = lax.axis_index("inner")
    outer = lax.axis_index("outer")
    quad = inner // 4
    active = inner % 4 < 3
    head = jnp.minimum(quad * 3 + inner % 4, HEADS - 1)

    def to_inner(src, dst, send, recv, target):
        return pltpu.make_async_remote_copy(
            src_ref=src, dst_ref=dst, send_sem=send, recv_sem=recv,
            device_id={"inner": target}, device_id_type=pl.DeviceIdType.MESH,
        )

    def to_outer(src, dst, send, recv, target):
        return pltpu.make_async_remote_copy(
            src_ref=src, dst_ref=dst, send_sem=send, recv_sem=recv,
            device_id={"outer": target}, device_id_type=pl.DeviceIdType.MESH,
        )

    loads = [
        pltpu.make_async_copy(src, dst, in_s.at[i])
        for i, (src, dst) in enumerate(
            [
                (om_hbm, om_ref), (ow_hbm, ow_ref), (q_hbm, q_ref), (g_hbm, g_ref),
                (k_hbm, k_ref), (v_hbm, v_ref), (o_hbm, o_ref),
            ]
        )
    ]
    barrier = pltpu.get_barrier_semaphore()

    for load in loads:
        load.start()

    def greet(d, _):
        pl.semaphore_signal(
            barrier, inc=1, device_id={"inner": (inner + d) % N}, device_id_type=pl.DeviceIdType.MESH
        )
        pl.semaphore_signal(
            barrier, inc=1, device_id={"outer": (outer + d) % N}, device_id_type=pl.DeviceIdType.MESH
        )
        return 0

    lax.fori_loop(1, N, greet, 0)
    for load in loads:
        load.wait()

    left = iota((1, 128), 1) < 64
    half_k = jnp.where(left, SCALE, 0.0).astype(BF)
    half_v = jnp.where(left, 0.0, 1.0).astype(BF)

    def block_of(u):
        return (quad // 2 + 1 - u // 2) % 2 * 2 + (quad + 1 - u % 2) % 2

    def peers():
        return [4 * block_of(i // 4) + (inner + i) % 4 for i in range(N) if i != 12]

    t_row = iota((T, 128), 0)
    t_lane = iota((T, 128), 1)
    place_m = onehot(t_lane == (t_row >> 2) + 64 * (inner % 2))
    place_w = onehot(t_lane == (t_row >> 6) + 4 * inner)
    tok = iota((1, T), 1)
    head_row = iota((16, 1), 0)
    om_col, ow_col = jnp.zeros((16, 1), I32), jnp.zeros((16, 1), I32)
    for h in range(HEADS):
        om_col = jnp.where(head_row == h, om_ref[h], om_col)
        ow_col = jnp.where(head_row == h, ow_ref[h], ow_col)
    keep_m = (tok & 3) == om_col
    keep_w = (tok & 63) == ow_col

    prod = g_ref[...].astype(F32) * o_ref[...].astype(F32)
    hi = prod.astype(BF)
    lo = (prod - hi.astype(F32)).astype(BF)
    of_head = onehot(iota((16, HEADS * 64), 0) == (iota((16, HEADS * 64), 1) >> 6))
    delta = nt(of_head, hi) + nt(of_head, lo)
    dl[...] = delta
    delta_m = nn(split3(jnp.where(keep_m, delta, 0.0)), place_m)
    delta_w = nn(split3(jnp.where(keep_w, delta, 0.0)), place_w)

    row16 = iota((16, 1), 0)
    for p in range(HEADS // 2):
        cols = pl.ds(p * 128, 128)
        qp, kp, vp, gp = q_ref[:, cols], k_ref[:, cols], v_ref[:, cols], g_ref[:, cols]
        for a in range(2):
            h = 2 * p + a
            b, c = 64 * a, 64 * a + 64
            x = jnp.concatenate([qp[:, b:c], gp[:, b:c]], axis=1)
            y = jnp.concatenate([kp[:, b:c], vp[:, b:c]], axis=1)
            xl[h] = x
            yl[h] = y
            om, ow = om_ref[h], ow_ref[h]
            row = iota((96, 1), 0)
            r = row - 64
            w = r & 15
            wide = jnp.where((r < 16) & (w < 4), 64 * w + ow, -1)
            wide = jnp.where((r >= 16) & (w >= 4) & (w < 8), 64 * (w - 4) + ow, wide)
            want = jnp.where(row < 64, 4 * row + om, wide)
            pick = onehot(iota((96, T), 1) == want)
            got = nn(pick, jnp.concatenate([x, y], axis=1))
            msg[h, 0:64, :] = got[0:64, 128:256].astype(BF)
            msg[h, 64:128, :] = got[0:64, 0:128].astype(BF)
            tile = got[64:80, 0:128] + got[80:96, 128:256]
            for i in range(3):
                tile = jnp.where(row16 == 8 + i, delta_m[16 * i + h : 16 * i + h + 1], tile)
                tile = jnp.where(row16 == 11 + i, delta_w[16 * i + h : 16 * i + h + 1], tile)
            msg_w[h] = tile.astype(BF)
    pl.semaphore_wait(barrier, 2 * (N - 1))

    def block_of(u):
        return (quad // 2 + 1 - u // 2) % 2 * 2 + (quad + 1 - u % 2) % 2

    def send_to_heads(src_of, dst, send, recv, rows=None):
        place = dst.at[inner] if rows is None else dst.at[inner, rows]
        for i in range(HEADS):
            block = block_of(i // 3)
            j = (i + inner) % 3
            h, target = 3 * block + j, 4 * block + j
            if i < 9:
                to_inner(src_of(h), place, send, recv, target).start()
            else:

                @pl.when(target != inner)
                def _():
                    to_inner(src_of(h), place, send, recv, target).start()

    def got_inner(dst, recv):
        to_inner(dst, dst, recv, recv, (inner + 1) % N).wait_recv()

    def got_outer(dst, recv):
        to_outer(dst, dst, recv, recv, (outer + 1) % N).wait_recv()

    def sent_inner(src, send):
        to_inner(src, src, send, send, (inner + 1) % N).wait_send()

    def sent_outer(src, send):
        to_outer(src, src, send, send, (outer + 1) % N).wait_send()

    send_to_heads(lambda h: msg_w.at[h], rx_w, mw_s, mw_r)
    send_to_heads(lambda h: msg.at[h, pl.ds(0, 64)], rx, mk_s, mk_r, pl.ds(0, 64))
    send_to_heads(lambda h: msg.at[h, pl.ds(64, 64)], rx, mq_s, mq_r.at[quad], pl.ds(64, 64))

    @pl.when(active)
    def _():
        rx_w[inner] = msg_w[head]
        rx[inner] = msg[head]

    top_l[...] = jnp.zeros((16, T), F32)
    sum_l[...] = jnp.ones((16, T), F32)

    def local_a(h, _):
        x, y = xl[h], yl[h]
        s = nt(y * half_k, x)
        top = jnp.max(s, axis=0, keepdims=True)
        e = jnp.exp(s - top)
        top_l[pl.ds(h, 1), :] = top
        sum_l[pl.ds(h, 1), :] = jnp.sum(e, axis=0, keepdims=True)
        d = nt(y * half_v, x)
        el[h] = e.astype(BF)
        gl[h] = (e * (d - dl[pl.ds(h, 1), :])).astype(BF)
        return 0

    lax.fori_loop(0, HEADS, local_a, 0, unroll=6)
    @pl.when(active)
    def _():
        got_inner(rx_w.at[pl.ds(0, N - 1)], mw_r)
        r, c = iota((144, T), 0), iota((144, T), 1)
        slot, owner = c & 15, c >> 4
        at = 16 * ((r & 63) >> 2) + (r & 3)
        j = r - 128
        take = jnp.where(r < 64, jnp.where(c == at, 1, 0), jnp.where(c == at + 4, 1, 0))
        in_m = jnp.where((slot >= 8) & (slot < 11) & ((owner >> 1) == j), 1, 0)
        in_w = jnp.where((slot >= 11) & (slot < 14) & (j == 8), 1, 0)
        take = jnp.where(r < 128, take, in_m + in_w)
        got = nn(onehot(take > 0), rx_w[...].reshape(T, 128))
        xw_w[...] = got[0:64].astype(BF)
        yw[...] = got[64:128].astype(BF)
        dm[...] = got[128:144]
        rxo[outer] = yw[...]
        for d in FAR:
            t = (outer + d) % N
            to_outer(yw, rxo.at[outer], yw_s, yw_r, t).start()

    lse_l = top_l[...] + jnp.log(sum_l[...])
    lse_m = sum3(nn(split3(jnp.where(keep_m, lse_l, 0.0)), place_m))
    lse_w = sum3(nn(split3(jnp.where(keep_w, lse_l, 0.0)), place_w))
    row8 = iota((8, 1), 0)
    for h in range(HEADS):
        st_tx[h] = jnp.where(row8 == 0, lse_m[h : h + 1], lse_w[h : h + 1])
    send_to_heads(lambda h: st_tx.at[h], st_rx, st_s, st_r)

    @pl.when(active)
    def _():
        st_rx[inner] = st_tx[head]

    def local_q(h, _):
        acc_q[h] = tn(gl[h], yl[h])
        where_kv[h] = onehot(iota((T, 64), 0) == 4 * iota((1, 64), 1) + om_ref[h])
        return 0

    lax.fori_loop(0, HEADS, local_q, 0, unroll=6)

    @pl.when(active)
    def _():
        got_inner(rx.at[pl.ds(0, N - 1), pl.ds(0, 64)], mk_r)
        om, ow = om_ref[head], ow_ref[head]
        yk[...] = rx[:, 0:64, :] * half_k
        yv[...] = rx[:, 0:64, :] * half_v

        x_w = xw_w[...]
        s = nt(yk[...].reshape(N * 64, 128), x_w)
        top = jnp.max(s, axis=0, keepdims=True)
        m_at_w = top + jnp.log(jnp.sum(jnp.exp(s - top), axis=0, keepdims=True))

        def mid_a(u):
            b = block_of(3 - u)
            got_inner(rx.at[pl.ds(0, 3 if u == 0 else 4), pl.ds(64, 64)], mq_r.at[b])
            x = rx[pl.ds(4 * b, 4), 64:128, :].reshape(T, 128)
            delta = jnp.concatenate([dm[pl.ds(2 * b, 1), :], dm[pl.ds(2 * b + 1, 1), :]], axis=1)
            top = jnp.full((1, T), NEG, F32)
            for kb in range(4):
                s = nt(yk[4 * kb : 4 * kb + 4].reshape(T, 128), x)
                s_scr[u, kb] = s
                top = jnp.maximum(top, jnp.max(s, axis=0, keepdims=True))
            total = jnp.zeros((1, T), F32)
            dq = jnp.zeros((T, 128), F32)
            for kb in range(4):
                e = jnp.exp(s_scr[u, kb] - top)
                total = total + jnp.sum(e, axis=0, keepdims=True)
                d = nt(yv[4 * kb : 4 * kb + 4].reshape(T, 128), x)
                em[b, kb] = e.astype(BF)
                g = (e * (d - delta)).astype(BF)
                gm[b, kb] = g
                dq = dq + tn(g, rx[4 * kb : 4 * kb + 4, 0:64, :].reshape(T, 128))
            for i in range(4):
                mine = dq[64 * i : 64 * i + 64]
                ret[4 * b + i, 64:96, :] = jnp.where(left, mine[:32], swap(mine[32:])).astype(BF)
            for i in range(2):
                mm[pl.ds(2 * b + i, 1), :] = top[:, 128 * i : 128 * i + 128]
                sm[pl.ds(2 * b + i, 1), :] = total[:, 128 * i : 128 * i + 128]
            for i in range(1 if u == 0 else 0, 4):
                t = 4 * b + (inner + i) % 4
                to_inner(ret.at[t, pl.ds(64, 32)], back.at[head, pl.ds(64, 32)], rq_s, rq_r, t).start()

        lane8, chunk8 = iota((8, 128), 1), iota((8, 128), 0)

        def share_lse():
            lse_m = mm[...] + jnp.log(sm[...])
            for j in range(8):
                ls_tx[j] = jnp.where(
                    chunk8 == 0, lse_m[j : j + 1], jnp.where(chunk8 == 1, lw[...], mm[j : j + 1, :])
                )
            for t in peers():
                to_inner(ls_tx.at[t // 2], ls_rx.at[head], ls_s, ls_r, t).start()
            ls_rx[head] = ls_tx[inner // 2]

        def wide(last):
            got_inner(st_rx.at[pl.ds(0, N - 1)], st_r)
            ones = onehot(iota((8, N), 0) == (iota((8, N), 1) >> 1))
            rows = st_rx[:, 0, :]
            first = rows.astype(BF).astype(F32)
            second = (rows - first).astype(BF).astype(F32)
            third = rows - first - second
            lm[...] = nn(ones, first.astype(BF)) + nn(ones, second.astype(BF)) + nn(ones, third.astype(BF))
            lse_local_w = jnp.sum(st_rx[:, 1, :], axis=0, keepdims=True)
            got_outer(rxo.at[pl.ds(0, N - 1)], yw_r)

            all_y = rxo[...].reshape(N * 64, 128)
            s = nt(all_y * half_k, x_w)
            top_w = jnp.max(s, axis=0, keepdims=True)
            e = jnp.exp(s - top_w)
            lse_w = top_w + jnp.log(jnp.sum(e, axis=0, keepdims=True))
            zeros64 = jnp.zeros((1, 64), F32)
            lw[...] = jnp.broadcast_to(jnp.concatenate([lse_w, zeros64], axis=1), (8, 128))
            if last:
                share_lse()
            d = nt(all_y * half_v, x_w)
            ew = e.astype(BF)
            gw = (e * (d - dm[8:9, 0:64])).astype(BF)
            shared = (ow & 3) == om
            spot = jnp.where(shared, ow >> 2, -1)
            spot_row = jnp.full((1, 64), spot, I32)
            total_w = lse3(lse_w, lse_local_w[:, :64], jnp.where(spot_row >= 0, m_at_w, NEG))
            weight_w = jnp.exp(top_w - total_w)
            col_w = jnp.broadcast_to(jnp.concatenate([weight_w, zeros64], axis=1), (128, 128)).T[0:64, 0:1]
            scaled = (x_w.astype(F32) * col_w).astype(BF)
            wp[...] = jnp.where(left, nn(gw, scaled), nn(ew, scaled)).astype(BF).reshape(N, 64, 128)
            rxp[outer] = wp[outer]

            for d in FAR:
                t = (outer + d) % N
                to_outer(wp.at[t], rxp.at[outer], wp_s, wp_r, t).start()

            dqw[...] = (tn(gw, all_y) * col_w).astype(BF)

            lse_w = lw[0:1, :]
            n128 = iota((128, 128), 1)
            spread = onehot(((n128 & 7) == (iota((128, 128), 0) >> 4)) & (n128 < 64))
            w_at_m = sum3(nt(split3(jnp.where((lane8 >> 3) == chunk8, lse_w, 0.0)), spread))
            wm[...] = jnp.where((lane8 & 15) == spot, w_at_m, NEG)

        late = outer >= 8
        for u in range(4):
            if u == 3:
                pl.when(late)(lambda: wide(False))
            mid_a(u)
        pl.when(late)(share_lse)
        pl.when(jnp.logical_not(late))(lambda: wide(True))

        lse_m = mm[...] + jnp.log(sm[...])
        weight_m = jnp.exp(mm[...] - lse3(lse_m, lm[...], wm[...]))
        columns = jnp.concatenate([weight_m, jnp.zeros((120, 128), F32)], axis=0).T
        for j in range(8):
            col = columns[:, j : j + 1]
            x = rx[2 * j : 2 * j + 2, 64:128, :].reshape(128, 128).astype(F32)
            xw_all[j // 2, 128 * (j % 2) : 128 * (j % 2) + 128, :] = (x * col).astype(BF)
        def mid_b(u, _):
            kb = block_of(u)
            from_g = jnp.zeros((T, 128), F32)
            from_e = jnp.zeros((T, 128), F32)
            for b in range(4):
                x = xw_all[b]
                from_g = from_g + nn(gm[b, kb], x)
                from_e = from_e + nn(em[b, kb], x)
            both = jnp.where(left, from_g, from_e).astype(BF)
            ret[pl.ds(4 * kb, 4), 0:64, :] = both.reshape(4, 64, 128)

            for j in range(4):
                t = 4 * kb + (inner + j) % 4

                @pl.when(t != inner)
                def _():
                    to_inner(ret.at[t, pl.ds(0, 64)], back.at[head, pl.ds(0, 64)], rk_s, rk_r, t).start()

            return 0

        lax.fori_loop(0, 4, mid_b, 0)
        back[head, 0:96, :] = ret[inner]

        got_outer(rxp.at[pl.ds(0, N - 1)], wp_r)
        kv_w = jnp.sum(rxp[...].astype(F32), axis=0).astype(BF)
        r256, n64 = iota((T, 64), 0), iota((T, 64), 1)
        slot = r256 & 15
        at = 4 * (r256 >> 4) + (slot & 3)
        rows_w = nn(onehot((n64 == at) & (slot < 4)), kv_w)
        rows_w = rows_w + nn(onehot((n64 == at) & (slot >= 4) & (slot < 8)), dqw[...])
        retw[...] = rows_w.astype(BF).reshape(N, 16, 128)

        for t in peers():
            to_inner(retw.at[t], back_w.at[head], rw_s, rw_r, t).start()
        back_w[head] = retw[inner]

    @pl.when(active)
    def _():
        got_inner(ls_rx.at[pl.ds(0, HEADS - 1)], ls_r)

    @pl.when(jnp.logical_not(active))
    def _():
        got_inner(ls_rx, ls_r)

    pad = jnp.zeros((4, 128), F32)
    lse_m = sum3(nt(split3(jnp.concatenate([ls_rx[:, 0, :], pad], axis=0)), place_m))
    lse_w = sum3(nt(split3(jnp.concatenate([ls_rx[:, 1, :], pad], axis=0)), place_w))
    total = lse3(lse_l, jnp.where(keep_m, lse_m, NEG), jnp.where(keep_w, lse_w, NEG))
    weight = jnp.exp(top_l[...] - total)
    top_m = sum3(nt(split3(jnp.concatenate([ls_rx[:, 2, :], pad], axis=0)), place_m))
    weight_m = jnp.where(keep_m, jnp.exp(jnp.where(keep_m, top_m, NEG) - total), 0.0)
    cols_l[...] = jnp.concatenate([weight, weight_m, jnp.zeros((96, T), F32)], axis=0).T
    for h in range(HEADS):
        col = cols_l[:, h : h + 1]
        x = (xl[h].astype(F32) * col).astype(BF)
        acc_kv[h] = jnp.where(left, nn(gl[h], x), nn(el[h], x))
        acc_q[h] = acc_q[h] * col
        col = cols_l[:, 16 + h : 17 + h]
        r = iota((1, 32), 1)
        t = iota((T, 32), 0)
        where_q[h, 0] = jnp.where(t == 4 * r + om_ref[h], col, 0.0).astype(BF)
        where_q[h, 1] = jnp.where(t == 4 * (r + 32) + om_ref[h], col, 0.0).astype(BF)

    c = iota((1, 192), 1)
    ow_c = jnp.zeros((1, 192), I32)
    for h in range(HEADS):
        ow_c = jnp.where((c >> 4) == h, ow_ref[h], ow_c)
    r = c & 15
    t = iota((T, 192), 0)
    places_w[0:T, :] = onehot(t == jnp.where(r < 4, 64 * r + ow_c, -1))
    places_w[T:, :] = onehot(t == jnp.where((r >= 4) & (r < 8), 64 * (r - 4) + ow_c, -1))

    @pl.when(active)
    def _():
        got_inner(back.at[pl.ds(0, HEADS - 1), pl.ds(64, 32)], rq_r)
        got_inner(back.at[pl.ds(0, HEADS - 1), pl.ds(0, 64)], rk_r)

    @pl.when(jnp.logical_not(active))
    def _():
        got_inner(back.at[pl.ds(0, HEADS), pl.ds(64, 32)], rq_r)
        got_inner(back.at[pl.ds(0, HEADS), pl.ds(0, 64)], rk_r)

    for p in range(HEADS // 2):
        cols = pl.ds(p * 128, 128)
        kvs, qs, rest = [], [], []
        for h in (2 * p, 2 * p + 1):
            kvs.append(acc_kv[h] + nn(where_kv[h], back[h, 0:64, :]))
            qs.append(acc_q[h] + nn(where_q[h, 0], back[h, 64:96, :]))
            rest.append(nn(where_q[h, 1], back[h, 64:96, :]))
        fin_q[:, cols] = jnp.where(left, qs[0] + swap(rest[0]), swap(qs[1]) + rest[1])
        fin_k[:, cols] = jnp.where(left, kvs[0], swap(kvs[1]))
        fin_v[:, cols] = jnp.where(left, swap(kvs[0]), kvs[1])

    def close(heads):
        got_inner(back_w.at[pl.ds(0, heads)], rw_r)
        sent_inner(msg_w.at[pl.ds(0, heads)], mw_s)
        sent_inner(msg.at[pl.ds(0, heads), pl.ds(0, 64)], mk_s)
        sent_inner(msg.at[pl.ds(0, heads), pl.ds(64, 64)], mq_s)
        sent_inner(st_rx.at[pl.ds(0, heads)], st_s)

    @pl.when(active)
    def _():
        close(HEADS - 1)
        sent_inner(st_rx.at[pl.ds(0, N - 1)], ls_s)
        sent_inner(ret.at[pl.ds(0, N - 1), pl.ds(64, 32)], rq_s)
        sent_inner(ret.at[pl.ds(0, N - 1), pl.ds(0, 64)], rk_s)
        sent_inner(retw.at[pl.ds(0, N - 1)], rw_s)
        sent_outer(rxo.at[pl.ds(0, N - 1)], yw_s)
        sent_outer(wp.at[pl.ds(0, N - 1)], wp_s)

    @pl.when(jnp.logical_not(active))
    def _():
        close(HEADS)


def finish(fin_q, fin_k, fin_v, back_w, places_w, dq_hbm, dk_hbm, dv_hbm, rk, rv, dq_ref, dk_ref, dv_ref, sems):
    left = iota((1, 128), 1) < 64
    rk[...] = jnp.zeros_like(rk)
    rv[...] = jnp.zeros_like(rv)
    for p in range(HEADS // 2):
        cols = pl.ds(p * 128, 128)
        a, b = back_w[2 * p].astype(F32), back_w[2 * p + 1].astype(F32)
        rk[32 * p : 32 * p + 16, cols] = jnp.where(left, a, 0.0).astype(BF)
        rk[32 * p + 16 : 32 * p + 32, cols] = jnp.where(left, 0.0, swap(b)).astype(BF)
        rv[32 * p : 32 * p + 16, cols] = jnp.where(left, swap(a), 0.0).astype(BF)
        rv[32 * p + 16 : 32 * p + 32, cols] = jnp.where(left, 0.0, b).astype(BF)
    copies = []
    for g in range(3):
        cols = pl.ds(256 * g, 256)
        kq = nn(places_w[...], rk[:, cols])
        dk_ref[:, cols] = (SCALE * (fin_k[:, cols] + kq[:T])).astype(BF)
        dq_ref[:, cols] = (SCALE * (fin_q[:, cols] + kq[T:])).astype(BF)
        dv_ref[:, cols] = (fin_v[:, cols] + nn(places_w[0:T, :], rv[:, cols])).astype(BF)
        for i, (src, dst) in enumerate([(dq_ref, dq_hbm), (dk_ref, dk_hbm), (dv_ref, dv_hbm)]):
            copies.append(pltpu.make_async_copy(src.at[:, cols], dst.at[:, cols], sems.at[i, g]))
            copies[-1].start()
    for copy in copies:
        copy.wait()


def per_device(queries, keys, values, saved_out, out_grad, offset_mid, offset_wide):
    vmem = pl.BlockSpec(memory_space=pltpu.VMEM)
    hbm = pl.BlockSpec(memory_space=pltpu.HBM)
    v = pltpu.VMEM
    dma = pltpu.SemaphoreType.DMA
    rows = jax.ShapeDtypeStruct((T, HEADS * 64), BF)
    parts = pl.pallas_call(
        kernel,
        out_shape=(
            jax.ShapeDtypeStruct((T, HEADS * 64), F32),
            jax.ShapeDtypeStruct((T, HEADS * 64), F32),
            jax.ShapeDtypeStruct((T, HEADS * 64), F32),
            jax.ShapeDtypeStruct((HEADS, 16, 128), BF),
            jax.ShapeDtypeStruct((2 * T, HEADS * 16), BF),
        ),
        in_specs=[hbm] * 7,
        out_specs=(vmem,) * 5,
        scratch_shapes=[
            pltpu.SMEM((HEADS,), I32),
            pltpu.SMEM((HEADS,), I32),
            v((T, HEADS * 64), BF),
            v((T, HEADS * 64), BF),
            v((T, HEADS * 64), BF),
            v((T, HEADS * 64), BF),
            v((T, HEADS * 64), BF),
            v((HEADS, T, 128), F32),
            v((HEADS, T, 128), F32),
            v((HEADS, BACK, 128), BF),
            v((HEADS, T, 64), BF),
            v((HEADS, 2, T, 32), BF),
            v((HEADS, T, 128), BF),
            v((HEADS, T, 128), BF),
            v((HEADS, 16, 128), BF),
            v((HEADS, 128, 128), BF),
            v((N, 16, 128), BF),
            v((N, 128, 128), BF),
            v((HEADS, T, T), BF),
            v((HEADS, T, T), BF),
            v((16, T), F32),
            v((16, T), F32),
            v((16, T), F32),
            v((T, 128), F32),
            v((HEADS, 8, 128), F32),
            v((N, 8, 128), F32),
            v((8, 8, 128), F32),
            v((HEADS, 8, 128), F32),
            v((N, 64, 128), BF),
            v((N, 64, 128), BF),
            v((4, 4, T, T), F32),
            v((4, 4, T, T), BF),
            v((4, 4, T, T), BF),
            v((8, 128), F32),
            v((8, 128), F32),
            v((16, 128), F32),
            v((8, 128), F32),
            v((8, 128), F32),
            v((4, T, 128), BF),
            v((64, 128), BF),
            v((64, 128), BF),
            v((N, 64, 128), BF),
            v((N, 64, 128), BF),
            v((N, 64, 128), BF),
            v((8, 128), F32),
            v((64, 128), BF),
            v((N, 96, 128), BF),
            v((N, 16, 128), BF),
            dma((7,)),
            dma, dma,
            dma, dma,
            dma, dma((4,)),
            dma, dma,
            dma, dma,
            dma, dma,
            dma, dma,
            dma, dma,
            dma, dma,
            dma, dma,
        ],
        compiler_params=pltpu.CompilerParams(
            collective_id=0, has_side_effects=True, vmem_limit_bytes=48 * 1024 * 1024
        ),
    )(
        *[
            pltpu.with_memory_space_constraint(x, pltpu.HBM)
            for x in (offset_mid, offset_wide, queries, keys, values, saved_out, out_grad)
        ]
    )
    return pl.pallas_call(
        finish,
        out_shape=(rows, rows, rows),
        in_specs=[vmem] * 5,
        out_specs=(hbm,) * 3,
        scratch_shapes=[v((HEADS * 16, HEADS * 64), BF)] * 2 + [v((T, HEADS * 64), BF)] * 3 + [dma((3, 3))],
        compiler_params=pltpu.CompilerParams(vmem_limit_bytes=40 * 1024 * 1024),
    )(*parts)


def solution(mesh):
    rows = P(("outer", "inner"), None)
    return jax.shard_map(
        per_device,
        mesh=mesh,
        in_specs=(rows, rows, rows, rows, rows, P(), P()),
        out_specs=(rows, rows, rows),
        check_vma=False,
    )
```
